256 devices in a mesh: tile: 64 (over z, y, core), slot: 4 (over x).
Axes of the slice: x: 4, y: 4, z: 8, core: 2. Of those that a mesh axis runs over, the one named last changes fastest.
Arguments:
- departure: bfloat16 [24576, 100], P(('tile', 'slot')), may hold values from -6 to 6
- inv_var: float32 [100], replicated, may hold values from 0.25 to 4
- k_matrix: bfloat16 [24576, 100, 411], P(('tile', 'slot')), may hold values from -0.625 to 0.625
- frac_row: bfloat16 [24576], P(('tile', 'slot')), may hold values from 0 to 1
- frac_col: bfloat16 [24576], P(('tile', 'slot')), may hold values from 0 to 1
- dest_tile: int32 [24576, 1], P(('tile', 'slot')), may hold values from 0 to 63; in each aligned block of 96 rows (0 to 95, 96 to 191, ...) at most 4 rows name the same one
- cell_row: int32 [24576], P(('tile', 'slot')), may hold values from 0 to 31
- cell_col: int32 [24576], P(('tile', 'slot')), may hold values from 0 to 254
- predictors: bfloat16 [24576, 8], P(('tile', 'slot')), may hold values from -6 to 6
- scan_pos: int32 [24576], P(('tile', 'slot')), may hold values from 0 to 119
Outputs:
- grid_adjoint: float32 [2048, 256, 411], P(('tile', 'slot'))
- bias_grad: float32 [100, 128], replicated
The draws below stay inside these ranges and needn't reach their ends.
Inputs may be any that keep to these rules, and one draw needn't show every extreme that they name: `dest_tile`: among the observations of one device, no tile is named by more than 4 of them, a bound that some block reaches.
All inputs are finite; a program needn't handle non-finite values.
Results may differ from the reference program's by a relative error of at most 0.004.
Values may be sent and summed in bfloat16 or wider, within the bound.
No kernel may reach another device: no remote copies, remote signals or barrier semaphores. Data moves between devices by JAX's collectives and lax.ppermute only.
A program may use at most 128 MiB of HBM per device.

```python
import math
import jax
import jax.numpy as jnp
import numpy as np
from jax import lax

CH = 100
NP = 8
NSCAN = 120
OBS_DEV = 96
GR = 32
GC = 256
VL = 411
CAP = 4
OBS = 24576
NROWS = 2048
N_TILE = 64


def touch_ends(drawn, stream_key, smallest, high):
    place = [jax.random.randint(jax.random.fold_in(stream_key, axis), (), 0, length) for axis, length in enumerate(drawn.shape)]
    main_axis = drawn.shape.index(max(drawn.shape))
    next_to = place[:main_axis] + [(place[main_axis] + 1) % drawn.shape[main_axis]] + place[main_axis + 1:]
    return drawn.at[tuple(place)].set(smallest).at[tuple(next_to)].set(high)


def block_scale(rng, extent, cuts, smallest, largest):
    gain, own = 1.0, jax.random.fold_in(rng, 6)
    for dim, shards_of in cuts:
        heights = jnp.exp(jax.random.uniform(jax.random.fold_in(own, dim), (shards_of,), jnp.float32, smallest / len(cuts), largest / len(cuts)))
        gain = gain * jnp.repeat(heights, extent[dim] // shards_of).reshape([-1 if axis == dim else 1 for axis in range(len(extent))])
    return gain


def assign_block(stream_key, own, number, rows, count, top, most, skew):
    sequence = jax.random.permutation(stream_key, count)
    packed, ordinary = shares(count, rows * top, most, skew, True), shares(count, rows * top, most, skew, False)
    places = jnp.arange(count)

    def named(lengths, rotation):
        used = int((lengths > 0).sum())
        fixed = max(1, used // 4)
        moved = fixed + (places - fixed + rotation * (used - fixed)) % max(1, count - fixed)
        return jnp.zeros((count,), jnp.int32).at[sequence[jnp.where(places < fixed, places, moved)]].set(jnp.asarray(lengths, jnp.int32))

    lengths = jnp.where(number % 4 == 0, named(packed, number // 4), named(ordinary, number - number // 4 - 1))
    mixed = jax.random.permutation(jax.random.fold_in(own, 3), count)
    source_of, sink = mixed[0:count // 2 * 2:2], mixed[1:count // 2 * 2:2]
    room = jnp.minimum(lengths[source_of] - 1, most - lengths[sink]) // 2
    room = jnp.where((source_of == sequence[0]) | (sink == sequence[0]) | (lengths[sink] == 0), 0, jnp.maximum(room, 0))
    moved = jax.random.randint(jax.random.fold_in(own, 4), (count // 2,), 0, 1 << 20) % (room + 1)
    lengths = lengths.at[source_of].add(-moved).at[sink].add(moved)
    labels = jnp.searchsorted(jnp.cumsum(lengths), jnp.arange(rows * top), side="right").astype(jnp.int32)
    listing = labels.reshape(top, rows).T
    listing = listing[jax.random.permutation(jax.random.fold_in(own, 1), rows)]
    rotation = jax.random.randint(jax.random.fold_in(own, 2), (rows, 1), 0, top)
    return jnp.take_along_axis(listing, (jnp.arange(top)[None, :] + rotation) % top, axis=1)


def shares(number_of, total, bound, slope, full):
    loads = [(1 << 20) // math.isqrt(rank ** slope) + 1 for rank in range(1, number_of + 1)]
    largest = bound if full else min(bound, max(-(-total // number_of), total * loads[0] // sum(loads)))
    least = 1 if total - largest >= number_of - 1 else 0
    given, surplus = [largest] + [least] * (number_of - 1), total - largest - least * (number_of - 1)
    while surplus > 0:
        movable = [i for i in range(1, number_of) if given[i] < largest] or [i for i in range(1, number_of) if given[i] < bound]
        pool, budget = sum([loads[i] for i in movable]), surplus
        for i in movable:
            extra = min(bound - given[i], max(1, budget * loads[i] // pool), surplus)
            given[i] = given[i] + extra
            surplus = surplus - extra
    return np.array(given)


def scatter_about(own_key, shape, width, limit, pieces=(), kind=jnp.bfloat16):
    loudness = block_scale(own_key, shape, pieces, -0.22, 0.18) if pieces else 1.0
    entries = jax.random.normal(own_key, shape, jnp.float32) * width * loudness
    return jnp.minimum(jnp.maximum(entries, -limit), limit).astype(kind)


def setup_inputs(seed: int = 0) -> dict:
    key_of = jax.random.split(jax.random.key(seed), 11)
    departure = scatter_about(key_of[0], (OBS, CH), 1.0, 6.0, ((0, 256),))
    inv_var = jnp.clip(jnp.exp(jax.random.uniform(key_of[1], (CH,), jnp.float32, math.log(0.25), math.log(4.0))), 0.25, 4.0)
    k_matrix = scatter_about(key_of[2], (OBS, CH, VL), CH ** -0.5, 0.625, ((0, 256),))
    frac_row = jnp.clip(1.0 * jax.random.uniform(key_of[3], (OBS,), jnp.float32) ** block_scale(key_of[3], (OBS,), ((0, 256),), -0.2, 0.2), 0.0, 1.0).astype(jnp.bfloat16)
    frac_col = jnp.clip(1.0 * jax.random.uniform(key_of[4], (OBS,), jnp.float32) ** block_scale(key_of[4], (OBS,), ((0, 256),), -0.2, 0.2), 0.0, 1.0).astype(jnp.bfloat16)
    dest_tile_keys = jax.random.split(jax.random.fold_in(key_of[5], 1), OBS // OBS_DEV)
    dest_tile_turns = jax.random.permutation(jax.random.fold_in(key_of[5], 3), OBS // OBS_DEV)
    dest_tile = jax.vmap(lambda own, number: assign_block(jax.random.fold_in(key_of[5], 2), own, number, OBS_DEV, N_TILE, 1, CAP, 2))(dest_tile_keys, dest_tile_turns).reshape((OBS, 1))
    cell_row = touch_ends(jax.random.randint(key_of[6], (OBS,), 0, GR), jax.random.fold_in(key_of[6], 1), 0, GR - 1).astype(jnp.int32)
    cell_col = touch_ends(jax.random.randint(key_of[7], (OBS,), 0, GC - 1), jax.random.fold_in(key_of[7], 1), 0, (GC - 1) - 1).astype(jnp.int32)
    predictors = scatter_about(key_of[8], (OBS, NP), 1.0, 6.0, ((0, 256),))
    scan_pos = touch_ends(jax.random.randint(key_of[9], (OBS,), 0, NSCAN), jax.random.fold_in(key_of[9], 1), 0, NSCAN - 1).astype(jnp.int32)
    return {"departure": departure, "inv_var": inv_var, "k_matrix": k_matrix, "frac_row": frac_row, "frac_col": frac_col, "dest_tile": dest_tile, "cell_row": cell_row, "cell_col": cell_col, "predictors": predictors, "scan_pos": scan_pos}


def reference(departure, inv_var, k_matrix, frac_row, frac_col, dest_tile, cell_row, cell_col, predictors, scan_pos):
    weighted = (departure.astype(jnp.float32) * inv_var[None, :]).astype(jnp.bfloat16)
    blocks = OBS // OBS_DEV

    def apply_block(pair):
        block_w, block_k = pair
        return jnp.einsum('oc,ocv->ov', block_w.astype(jnp.float32), block_k.astype(jnp.float32)).astype(jnp.bfloat16)
    profile = lax.map(apply_block, (weighted.reshape(blocks, OBS_DEV, CH), k_matrix.reshape(blocks, OBS_DEV, CH, VL)))
    profile = profile.reshape(OBS, VL).astype(jnp.float32)
    row_frac = frac_row.astype(jnp.float32)
    col_frac = frac_col.astype(jnp.float32)
    lower = dest_tile[:, 0] * GR + cell_row
    upper = (lower + 1) % NROWS
    indices = jnp.concatenate([lower * GC + cell_col, lower * GC + cell_col + 1, upper * GC + cell_col, upper * GC + cell_col + 1])
    weights = jnp.concatenate([(1.0 - row_frac) * (1.0 - col_frac), (1.0 - row_frac) * col_frac, row_frac * (1.0 - col_frac), row_frac * col_frac])
    values = weights[:, None] * jnp.concatenate([profile, profile, profile, profile], 0)
    column_grid = jnp.zeros((NROWS * GC, VL), jnp.float32).at[indices].add(values).reshape(NROWS, GC, VL)
    indicator = (scan_pos[:, None] == jnp.arange(NSCAN, dtype=jnp.int32)[None, :]).astype(jnp.bfloat16)
    basis_rows = jnp.concatenate([predictors, indicator], 1)
    bias_sum = lax.dot_general(weighted, basis_rows, (((0,), (0,)), ((), ())), preferred_element_type=jnp.float32)
    return (column_grid, bias_sum / math.sqrt(OBS))
```

```python
import functools
import math

import jax
import jax.numpy as jnp
from jax import lax
from jax.experimental import pallas as pl
from jax.experimental.pallas import tpu as pltpu
from jax.sharding import PartitionSpec as P

F32 = jnp.float32
BF16 = jnp.bfloat16
NT = (((1,), (1,)), ((), ()))
NN = (((1,), (0,)), ((), ()))

CAP = 4
GR = 32
GC = 256
LANES = 512
VROWS = 432
VCHUNK = 48
CHUNK_ROW = 416
BLOCK = 8
VMEM = 48 * 1024 * 1024


def iota(shape, dim):
    return lax.broadcasted_iota(jnp.int32, shape, dim)


def dot(a, b, dims):
    return lax.dot_general(a, b, dims, preferred_element_type=F32)


def ones_where(mask):
    return jnp.where(mask, 1.0, 0.0).astype(BF16)


def send_kernel(dep, inv, k_hbm, tile, frow, fcol, crow, ccol, predt, scan, out, kbuf, acc, sems, *, steps):
    chans, obs, levels = k_hbm.shape
    per = chans // steps
    copies = [
        pltpu.make_async_copy(k_hbm.at[pl.ds(i * per, per)], kbuf.at[pl.ds(i * per, per)], sems.at[i])
        for i in range(steps)
    ]
    for copy in copies:
        copy.start()
    slots = out.shape[0]
    wbf = (dep[...].astype(F32) * inv[...]).astype(BF16)
    w = wbf.astype(F32)

    tr = jnp.broadcast_to(tile[...].astype(F32), (obs, obs))
    ri, ci = iota((obs, obs), 0), iota((obs, obs), 1)
    tc = jnp.sum(jnp.where(ri == ci, tr, 0.0), 1, keepdims=True)
    rank = jnp.sum(jnp.where((tc == tr) & (ri < ci), 1.0, 0.0), 0, keepdims=True)
    slot = (tile[...].astype(F32) * CAP + rank).astype(jnp.int32)
    sel = ones_where(iota((slots, obs), 0) == slot)

    base = levels - (LANES - 128)
    rows = iota((128, obs), 0)
    place = jnp.where(rows == base, frow[...].astype(F32), 0.0)
    place = jnp.where(rows == base + 1, fcol[...].astype(F32), place)
    place = jnp.where(rows == base + 2, crow[...].astype(F32), place)
    place = jnp.where(rows == base + 3, ccol[...].astype(F32), place)
    extra = dot(sel, place.astype(BF16), NT)

    npred = predt.shape[0]
    kinds = 128
    ind = jnp.where(iota((kinds - npred, obs), 0) == scan[...], 1.0, 0.0)
    basist = jnp.concatenate([predt[...].astype(F32), ind], 0).astype(BF16)
    biast = dot(basist, wbf, NN)
    hi = biast.astype(BF16)
    lo = (biast - hi.astype(F32)).astype(BF16)
    half = chans // 2
    first = base + 4
    er, ec = iota((chans, 128), 0), iota((chans, 128), 1)
    parts = []
    for h in range(2):
        e = ones_where((ec == er - h * half + first) & (er >= h * half) & (er < (h + 1) * half))
        f = ones_where((ec == er - h * half + first + half) & (er >= h * half) & (er < (h + 1) * half))
        parts.append(dot(hi, e, NN) + dot(lo, f, NN))
    extra = extra + jnp.concatenate(parts, 0)

    acc[...] = jnp.zeros(acc.shape, F32)
    for i in range(steps):
        copies[i].wait()
        for r in range(0, obs, 16):
            total = acc[r : r + 16, 0:levels]
            for c in range(i * per, (i + 1) * per):
                total = total + w[r : r + 16, c : c + 1] * kbuf[c, r : r + 16, :].astype(F32)
            acc[r : r + 16, 0:levels] = total
    placed = dot(sel, acc[...].astype(BF16), NN)
    out[:, 0 : LANES - 128] = placed[:, 0 : LANES - 128].astype(BF16)
    out[:, LANES - 128 : LANES] = (placed[:, LANES - 128 : LANES] + extra).astype(BF16)


def turn_kernel(got, out, *, levels, half):
    slots = got.shape[0]
    out[0:CHUNK_ROW, :] = jnp.transpose(got[...].astype(F32))[0:CHUNK_ROW, :].astype(BF16)
    pick = ones_where(iota((8, slots), 1) % CAP == iota((8, slots), 0))
    total = dot(pick, got[:, LANES - 128 : LANES], NN)
    first = levels - (LANES - 128) + 4
    lane = iota((8, 128), 1)
    kept = 128 - first - half
    chunk = jnp.where(lane < half, pltpu.roll(total, 128 - first, 1), 0.0)
    chunk = chunk + jnp.where(lane < kept, pltpu.roll(total, 128 - first - half, 1), 0.0)
    high = chunk.astype(BF16).astype(F32)
    both = jnp.concatenate([high, chunk - high], 0)
    out[CHUNK_ROW:VROWS, 0:128] = both.astype(BF16)
    out[CHUNK_ROW:VROWS, 128:slots] = jnp.zeros((VROWS - CHUNK_ROW, slots - 128), BF16)


def coords_of(refs, levels, k):
    tops = [ref[CHUNK_ROW - 16 : CHUNK_ROW, :].astype(F32) for ref in refs]
    at = levels + k - (CHUNK_ROW - 16)
    return jnp.concatenate([top[at : at + 1, :] for top in tops], 1)


def prep_kernel(first_row, a0, a1, a2, a3, spill, colw, roww, chunk, *, levels):
    refs = (a0, a1, a2, a3)
    total = sum([r[CHUNK_ROW : CHUNK_ROW + 16, 0:128].astype(F32) for r in refs])
    chunk[...] = total[0:8, :] + total[8:16, :]
    fr, fc, cr, cc = [coords_of(refs, levels, k) for k in range(4)]
    n = fr.shape[1]
    cols = iota((GC, n), 0)
    at = cc.astype(jnp.int32)
    cw = jnp.where(cols == at, 1.0 - fc, 0.0) + jnp.where(cols == at + 1, fc, 0.0)
    cw = cw.astype(BF16)
    colw[...] = cw
    row = cr.astype(jnp.int32)
    rel = iota((BLOCK, n), 0) + first_row[0]
    roww[...] = jnp.where(rel == row, 1.0 - fr, 0.0) + jnp.where(rel == row + 1, fr, 0.0)
    last = jnp.where(row == GR - 1, fr, 0.0)
    part = a0.shape[1]
    out = jnp.zeros((CHUNK_ROW, GC), F32)
    for j, ref in enumerate(refs):
        lhs = (ref[0:CHUNK_ROW, :].astype(F32) * last[:, j * part : (j + 1) * part]).astype(BF16)
        out = out + dot(lhs, cw[:, j * part : (j + 1) * part], NT)
    spill[0:CHUNK_ROW, :] = out.astype(BF16)
    spill[CHUNK_ROW:VROWS, :] = jnp.zeros((VROWS - CHUNK_ROW, GC), BF16)


def grid_kernel(a0, a1, a2, a3, colw, roww, spill, out):
    part = a0.shape[1]
    total = jnp.zeros((VCHUNK * BLOCK, GC), F32)
    for j, ref in enumerate((a0, a1, a2, a3)):
        cols = slice(j * part, (j + 1) * part)
        lhs = ref[...].astype(F32)[:, None, :] * roww[:, cols][None, :, :]
        lhs = lhs.reshape(VCHUNK * BLOCK, part).astype(BF16)
        total = total + dot(lhs, colw[:, cols], NT)
    total = total.reshape(VCHUNK, BLOCK, GC)
    first = iota((VCHUNK, BLOCK, GC), 1) == 0
    out[...] = total + jnp.where(first, spill[...].astype(F32)[:, None, :], 0.0)


def bias_kernel(got, out, *, half, scale):
    t = jnp.transpose(got[...])
    n = got.shape[0] // 2
    out[0:half, :] = t[0:half, 0:n] * scale
    out[half : 2 * half, :] = t[0:half, n : 2 * n] * scale


def whole(shape):
    return pl.BlockSpec(shape, lambda *_: (0,) * len(shape))


VM = pl.BlockSpec(memory_space=pltpu.VMEM)


def per_device(
    departure, inv_var, k_matrix, frac_row, frac_col, dest_tile, cell_row, cell_col, predictors, scan_pos
):
    n_tile = lax.axis_size("tile")
    n_slot = lax.axis_size("slot")
    obs, chans, levels = k_matrix.shape
    slots = n_tile * CAP
    params = pltpu.CompilerParams(vmem_limit_bytes=VMEM)
    steps = 10
    flat = lambda x: x.reshape(1, obs)
    send = pl.pallas_call(
        functools.partial(send_kernel, steps=steps),
        out_shape=jax.ShapeDtypeStruct((slots, LANES), BF16),
        in_specs=[VM, VM, pl.BlockSpec(memory_space=pl.ANY)] + [VM] * 7,
        out_specs=VM,
        scratch_shapes=[
            pltpu.VMEM((chans, obs, levels), BF16),
            pltpu.VMEM((obs, LANES), F32),
            pltpu.SemaphoreType.DMA((steps,)),
        ],
        compiler_params=params,
        name="send",
    )(
        departure,
        inv_var.reshape(1, chans),
        jnp.transpose(k_matrix, (1, 0, 2)),
        flat(dest_tile),
        flat(frac_row),
        flat(frac_col),
        flat(cell_row),
        flat(cell_col),
        predictors.T,
        flat(scan_pos),
    )
    got = lax.all_to_all(send.reshape(n_tile, CAP, LANES), "tile", 0, 0, tiled=True)
    turned = pl.pallas_call(
        functools.partial(turn_kernel, levels=levels, half=chans // 2),
        out_shape=jax.ShapeDtypeStruct((VROWS, slots), BF16),
        in_specs=[VM],
        out_specs=VM,
        compiler_params=params,
        name="turn",
    )(got.reshape(slots, LANES))
    blocks = [turned] + [
        lax.ppermute(turned, "slot", [(i, (i + d) % n_slot) for i in range(n_slot)]) for d in (1, 3, 2)
    ]
    total = n_slot * slots
    first_row = (lax.axis_index("slot") * BLOCK).astype(jnp.int32).reshape(1)
    spill, colw, roww, chunk = pl.pallas_call(
        functools.partial(prep_kernel, levels=levels),
        out_shape=(
            jax.ShapeDtypeStruct((VROWS, GC), BF16),
            jax.ShapeDtypeStruct((GC, total), BF16),
            jax.ShapeDtypeStruct((BLOCK, total), F32),
            jax.ShapeDtypeStruct((8, 128), F32),
        ),
        in_specs=[pl.BlockSpec(memory_space=pltpu.SMEM)] + [VM] * 4,
        out_specs=(VM,) * 4,
        compiler_params=params,
        name="prep",
    )(first_row, *blocks)
    pairs = [(t * n_slot, ((t + 1) % n_tile) * n_slot) for t in range(n_tile)]
    arrived = lax.ppermute(spill, ("tile", "slot"), pairs)
    chunks = jnp.broadcast_to(chunk[None, 0:CAP, :], (n_tile, CAP, 128))
    chunks = lax.all_to_all(chunks, "tile", 0, 0, tiled=True).reshape(slots, 128)
    grid = pl.pallas_call(
        grid_kernel,
        grid=(VROWS // VCHUNK,),
        out_shape=jax.ShapeDtypeStruct((levels, BLOCK, GC), F32),
        in_specs=[pl.BlockSpec((VCHUNK, slots), lambda i: (i, 0))] * 4
        + [whole((GC, total)), whole((BLOCK, total)), pl.BlockSpec((VCHUNK, GC), lambda i: (i, 0))],
        out_specs=pl.BlockSpec((VCHUNK, BLOCK, GC), lambda i: (i, 0, 0)),
        compiler_params=params,
        name="grid",
    )(*blocks, colw, roww, arrived)
    bias = pl.pallas_call(
        functools.partial(bias_kernel, half=chans // 2, scale=1.0 / math.sqrt(obs * n_tile * n_slot)),
        out_shape=jax.ShapeDtypeStruct((chans, 128), F32),
        in_specs=[VM],
        out_specs=VM,
        compiler_params=params,
        name="bias",
    )(chunks)
    return jnp.transpose(grid, (1, 2, 0)), bias


def solution(mesh):
    both = ("tile", "slot")
    placed = (
        P(both, None),
        P(),
        P(both, None, None),
        P(both),
        P(both),
        P(both, None),
        P(both),
        P(both),
        P(both, None),
        P(both),
    )
    return jax.shard_map(
        per_device,
        mesh=mesh,
        in_specs=placed,
        out_specs=(P(both, None, None), P()),
        check_vma=False,
    )
```

```python
import functools
import math

import jax
import jax.numpy as jnp
from jax import lax
from jax.experimental import pallas as pl
from jax.experimental.pallas import tpu as pltpu
from jax.sharding import PartitionSpec as P

F32 = jnp.float32
BF16 = jnp.bfloat16
NT = (((1,), (1,)), ((), ()))
NN = (((1,), (0,)), ((), ()))

CAP = 4
GR = 32
GC = 256
LANES = 512
VROWS = 416
VCHUNK = 104
BLOCK = 8
VMEM = 48 * 1024 * 1024


def iota(shape, dim):
    return lax.broadcasted_iota(jnp.int32, shape, dim)


def dot(a, b, dims):
    return lax.dot_general(a, b, dims, preferred_element_type=F32)


def ones_where(mask):
    return jnp.where(mask, 1.0, 0.0).astype(BF16)


def send_kernel(*refs, steps):
    k_hbm, small_hbm, out, small, kbuf, acc, sems, small_sems = refs[0], refs[1:10], *refs[10:11], refs[11:20], *refs[20:]
    chans, obs, levels = k_hbm.shape
    per = chans // steps
    small_copies = [
        pltpu.make_async_copy(src, dst, small_sems.at[i]) for i, (src, dst) in enumerate(zip(small_hbm, small))
    ]
    for copy in small_copies:
        copy.start()
    copies = [
        pltpu.make_async_copy(k_hbm.at[pl.ds(i * per, per)], kbuf.at[pl.ds(i * per, per)], sems.at[i])
        for i in range(steps)
    ]
    for copy in copies:
        copy.start()
    for copy in small_copies:
        copy.wait()
    dep, inv, tile, frow, fcol, crow, ccol, predt, scan = small
    slots = out.shape[0]
    wbf = (dep[...].astype(F32) * inv[...]).astype(BF16)
    w = wbf.astype(F32)

    tr = jnp.broadcast_to(tile[...].astype(F32), (obs, obs))
    ri, ci = iota((obs, obs), 0), iota((obs, obs), 1)
    tc = jnp.sum(jnp.where(ri == ci, tr, 0.0), 1, keepdims=True)
    rank = jnp.sum(jnp.where((tc == tr) & (ri < ci), 1.0, 0.0), 0, keepdims=True)
    slot = (tile[...].astype(F32) * CAP + rank).astype(jnp.int32)
    sel = ones_where(iota((slots, obs), 0) == slot)

    base = levels - (LANES - 128)
    rows = iota((128, obs), 0)
    place = jnp.where(rows == base, frow[...].astype(F32), 0.0)
    place = jnp.where(rows == base + 1, fcol[...].astype(F32), place)
    place = jnp.where(rows == base + 2, crow[...].astype(F32), place)
    place = jnp.where(rows == base + 3, ccol[...].astype(F32), place)
    extra = dot(sel, place.astype(BF16), NT)

    npred = predt.shape[0]
    kinds = 128
    ind = jnp.where(iota((kinds - npred, obs), 0) == scan[...], 1.0, 0.0)
    basist = jnp.concatenate([predt[...].astype(F32), ind], 0).astype(BF16)
    biast = dot(basist, wbf, NN)
    hi = biast.astype(BF16)
    lo = (biast - hi.astype(F32)).astype(BF16)
    half = chans // 2
    first = base + 4
    er, ec = iota((chans, 128), 0), iota((chans, 128), 1)
    parts = []
    for h in range(2):
        e = ones_where((ec == er - h * half + first) & (er >= h * half) & (er < (h + 1) * half))
        f = ones_where((ec == er - h * half + first + half) & (er >= h * half) & (er < (h + 1) * half))
        parts.append(dot(hi, e, NN) + dot(lo, f, NN))
    extra = extra + jnp.concatenate(parts, 0)

    acc[...] = jnp.zeros(acc.shape, F32)
    for i in range(steps):
        copies[i].wait()
        for r in range(0, obs, 16):
            total = acc[r : r + 16, 0:levels]
            for c in range(i * per, (i + 1) * per):
                total = total + w[r : r + 16, c : c + 1] * kbuf[c, r : r + 16, :].astype(F32)
            acc[r : r + 16, 0:levels] = total
    placed = dot(sel, acc[...].astype(BF16), NN)
    out[:, 0 : LANES - 128] = placed[:, 0 : LANES - 128].astype(BF16)
    out[:, LANES - 128 : LANES] = (placed[:, LANES - 128 : LANES] + extra).astype(BF16)


def turn_kernel(got, out, chunk, *, levels, half):
    slots = got.shape[0]
    out[...] = jnp.transpose(got[...].astype(F32))[0:VROWS, :].astype(BF16)
    pick = ones_where(iota((slots, slots), 1) % CAP == iota((slots, slots), 0) % CAP)
    total = dot(pick, got[:, LANES - 128 : LANES], NN)
    first = levels - (LANES - 128) + 4
    lane = iota((slots, 128), 1)
    kept = 128 - first - half
    sums = jnp.where(lane < half, pltpu.roll(total, 128 - first, 1), 0.0)
    chunk[...] = sums + jnp.where(lane < kept, pltpu.roll(total, 128 - first - half, 1), 0.0)


def prep_kernel(first_row, a0, a1, a2, a3, spill, colw, roww, *, levels):
    refs = (a0, a1, a2, a3)
    tops = jnp.concatenate([ref[VROWS - 16 : VROWS, :].astype(F32) for ref in refs], 1)
    at = levels - (VROWS - 16)
    fr, cr = tops[at : at + 1, :], tops[at + 2 : at + 3, :]
    n = fr.shape[1]
    turned = jnp.transpose(tops)
    fc, cc = turned[:, at + 1 : at + 2], turned[:, at + 3 : at + 4].astype(jnp.int32)
    cols = iota((n, GC), 1)
    cw = jnp.where(cols == cc, 1.0 - fc, jnp.where(cols == cc + 1, fc, 0.0)).astype(BF16)
    colw[...] = cw
    row = cr.astype(jnp.int32)
    rel = iota((BLOCK, n), 0) + first_row[0]
    roww[...] = jnp.where(rel == row, 1.0 - fr, 0.0) + jnp.where(rel == row + 1, fr, 0.0)
    last = jnp.where(row == GR - 1, fr, 0.0)
    part = a0.shape[1]
    out = jnp.zeros((VROWS, GC), F32)
    for j, ref in enumerate(refs):
        lhs = (ref[...].astype(F32) * last[:, j * part : (j + 1) * part]).astype(BF16)
        out = out + dot(lhs, cw[j * part : (j + 1) * part, :], NN)
    spill[...] = out.astype(BF16)


def grid_kernel(a0, a1, a2, a3, colw, roww, spill, out):
    part = a0.shape[1]
    total = jnp.zeros((VCHUNK * BLOCK, GC), F32)
    for j, ref in enumerate((a0, a1, a2, a3)):
        cols = slice(j * part, (j + 1) * part)
        lhs = ref[...].astype(F32)[:, None, :] * roww[:, cols][None, :, :]
        lhs = lhs.reshape(VCHUNK * BLOCK, part).astype(BF16)
        total = total + dot(lhs, colw[cols, :], NN)
    total = total.reshape(VCHUNK, BLOCK, GC)
    first = iota((VCHUNK, BLOCK, GC), 1) == 0
    out[...] = total + jnp.where(first, spill[...].astype(F32)[:, None, :], 0.0)


def slot_bias_kernel(got, out, *, half):
    t = jnp.transpose(got[...])
    n = got.shape[0] // 2
    out[0:half, :] = t[0:half, 0:n]
    out[half : 2 * half, :] = t[0:half, n : 2 * n]


def bias_kernel(b0, b1, b2, b3, out, *, scale):
    out[...] = ((b0[...] + b1[...]) + (b2[...] + b3[...])) * scale


def whole(shape):
    return pl.BlockSpec(shape, lambda *_: (0,) * len(shape))


VM = pl.BlockSpec(memory_space=pltpu.VMEM)
HBM = pl.BlockSpec(memory_space=pltpu.HBM)


def per_device(
    departure, inv_var, k_matrix, frac_row, frac_col, dest_tile, cell_row, cell_col, predictors, scan_pos
):
    n_tile = lax.axis_size("tile")
    n_slot = lax.axis_size("slot")
    obs, chans, levels = k_matrix.shape
    slots = n_tile * CAP
    params = pltpu.CompilerParams(vmem_limit_bytes=VMEM)
    tight = pltpu.CompilerParams(vmem_limit_bytes=56 * 1024 * 1024)
    steps = 10
    flat = lambda x: x.reshape(1, obs)
    small = (
        departure,
        inv_var.reshape(1, chans),
        flat(dest_tile),
        flat(frac_row),
        flat(frac_col),
        flat(cell_row),
        flat(cell_col),
        predictors.T,
        flat(scan_pos),
    )
    send = pl.pallas_call(
        functools.partial(send_kernel, steps=steps),
        out_shape=jax.ShapeDtypeStruct((slots, LANES), BF16),
        in_specs=[HBM] * (1 + len(small)),
        out_specs=VM,
        scratch_shapes=[pltpu.VMEM(x.shape, x.dtype) for x in small]
        + [
            pltpu.VMEM((chans, obs, levels), BF16),
            pltpu.VMEM((obs, LANES), F32),
            pltpu.SemaphoreType.DMA((steps,)),
            pltpu.SemaphoreType.DMA((len(small),)),
        ],
        compiler_params=tight,
        name="send",
    )(jnp.transpose(k_matrix, (1, 0, 2)), *small)
    got = lax.all_to_all(send.reshape(n_tile, CAP, LANES), "tile", 0, 0, tiled=True)
    turned, chunk = pl.pallas_call(
        functools.partial(turn_kernel, levels=levels, half=chans // 2),
        out_shape=(jax.ShapeDtypeStruct((VROWS, slots), BF16), jax.ShapeDtypeStruct((slots, 128), F32)),
        in_specs=[VM],
        out_specs=(VM, VM),
        compiler_params=params,
        name="turn",
    )(got.reshape(slots, LANES))

    def around(x):
        return [x] + [lax.ppermute(x, "slot", [(i, (i + d) % n_slot) for i in range(n_slot)]) for d in (1, 3, 2)]

    blocks = around(turned)
    chunks = lax.all_to_all(chunk.reshape(n_tile, CAP, 128), "tile", 0, 0, tiled=True).reshape(slots, 128)
    total = n_slot * slots
    first_row = (lax.axis_index("slot") * BLOCK).astype(jnp.int32).reshape(1)
    spill, colw, roww = pl.pallas_call(
        functools.partial(prep_kernel, levels=levels),
        out_shape=(
            jax.ShapeDtypeStruct((VROWS, GC), BF16),
            jax.ShapeDtypeStruct((total, GC), BF16),
            jax.ShapeDtypeStruct((BLOCK, total), F32),
        ),
        in_specs=[pl.BlockSpec(memory_space=pltpu.SMEM)] + [VM] * 4,
        out_specs=(VM,) * 3,
        compiler_params=params,
        name="prep",
    )(first_row, *blocks)
    pairs = [(t * n_slot, ((t + 1) % n_tile) * n_slot) for t in range(n_tile)]
    arrived = lax.ppermute(spill, ("tile", "slot"), pairs)
    slot_bias = pl.pallas_call(
        functools.partial(slot_bias_kernel, half=chans // 2),
        out_shape=jax.ShapeDtypeStruct((chans, 128), F32),
        in_specs=[VM],
        out_specs=VM,
        compiler_params=params,
        name="slot_bias",
    )(chunks)
    biases = around(slot_bias)
    grid = pl.pallas_call(
        grid_kernel,
        grid=(VROWS // VCHUNK,),
        out_shape=jax.ShapeDtypeStruct((levels, BLOCK, GC), F32),
        in_specs=[pl.BlockSpec((VCHUNK, slots), lambda i: (i, 0))] * 4
        + [whole((total, GC)), whole((BLOCK, total)), pl.BlockSpec((VCHUNK, GC), lambda i: (i, 0))],
        out_specs=pl.BlockSpec((VCHUNK, BLOCK, GC), lambda i: (i, 0, 0)),
        compiler_params=params,
        cost_estimate=pl.CostEstimate(
            flops=2 * levels * BLOCK * GC * total, bytes_accessed=16 * levels * BLOCK * GC, transcendentals=0
        ),
        name="grid",
    )(*blocks, colw, roww, arrived)
    *biases, grid = lax.optimization_barrier((*biases, grid))
    bias = pl.pallas_call(
        functools.partial(bias_kernel, scale=1.0 / math.sqrt(obs * n_tile * n_slot)),
        out_shape=jax.ShapeDtypeStruct((chans, 128), F32),
        in_specs=[VM] * 4,
        out_specs=VM,
        compiler_params=params,
        name="bias",
    )(*biases)
    return jnp.transpose(grid, (1, 2, 0)), bias


def solution(mesh):
    both = ("tile", "slot")
    placed = (
        P(both, None),
        P(),
        P(both, None, None),
        P(both),
        P(both),
        P(both, None),
        P(both),
        P(both),
        P(both, None),
        P(both),
    )
    return jax.shard_map(
        per_device,
        mesh=mesh,
        in_specs=placed,
        out_specs=(P(both, None, None), P()),
        check_vma=False,
    )
```

```python
import functools
import math

import jax
import jax.numpy as jnp
from jax import lax
from jax.experimental import pallas as pl
from jax.experimental.pallas import tpu as pltpu
from jax.sharding import PartitionSpec as P

F32 = jnp.float32
BF16 = jnp.bfloat16
NT = (((1,), (1,)), ((), ()))
NN = (((1,), (0,)), ((), ()))

CAP = 4
GR = 32
GC = 256
LANES = 512
WIDE = LANES // 2
VROWS = 416
VCHUNK = 104
BLOCK = 8
VMEM = 24 * 1024 * 1024


def iota(shape, dim):
    return lax.broadcasted_iota(jnp.int32, shape, dim)


def dot(a, b, dims):
    return lax.dot_general(a, b, dims, preferred_element_type=F32)


def ones_where(mask):
    return jnp.where(mask, 1.0, 0.0).astype(BF16)


def send_kernel(*refs, steps):
    k_hbm, small_hbm, out, small, kbuf, acc, sems, small_sems = refs[0], refs[1:10], *refs[10:11], refs[11:20], *refs[20:]
    chans, obs, levels = k_hbm.shape
    per = chans // steps
    small_copies = [
        pltpu.make_async_copy(src, dst, small_sems.at[i]) for i, (src, dst) in enumerate(zip(small_hbm, small))
    ]
    copies = [
        pltpu.make_async_copy(k_hbm.at[pl.ds(i * per, per)], kbuf.at[pl.ds(i * per, per)], sems.at[i])
        for i in range(steps)
    ]
    for copy in small_copies[:2] + copies[:2] + small_copies[2:] + copies[2:]:
        copy.start()
    dep, inv, tile, frow, fcol, crow, ccol, predt, scan = small
    rows_out = out.shape[0]
    for copy in small_copies[:2]:
        copy.wait()
    wbf = (dep[...].astype(F32) * inv[...]).astype(BF16)
    w = wbf.astype(F32)

    def sums(i):
        copies[i].wait()
        for r in range(0, obs, 16):
            total = acc[r : r + 16, 0:levels]
            for c in range(i * per, (i + 1) * per):
                total = total + w[r : r + 16, c : c + 1] * kbuf[c, r : r + 16, :].astype(F32)
            acc[r : r + 16, 0:levels] = total

    acc[...] = jnp.zeros(acc.shape, F32)
    for i in range(steps // 2):
        sums(i)
    for copy in small_copies[2:]:
        copy.wait()

    tr = jnp.broadcast_to(tile[...].astype(F32), (obs, obs))
    ri, ci = iota((obs, obs), 0), iota((obs, obs), 1)
    tc = jnp.sum(jnp.where(ri == ci, tr, 0.0), 1, keepdims=True)
    rank = jnp.sum(jnp.where((tc == tr) & (ri < ci), 1.0, 0.0), 0, keepdims=True)
    slot = (tile[...].astype(F32) * (2 * CAP) + rank).astype(jnp.int32)
    at = iota((rows_out, obs), 0)
    first_half, second_half = ones_where(at == slot), ones_where(at == slot + CAP)

    base = levels - (LANES - 128)
    rows = iota((128, obs), 0)
    place = jnp.where(rows == base, frow[...].astype(F32), 0.0)
    place = jnp.where(rows == base + 1, fcol[...].astype(F32), place)
    place = jnp.where(rows == base + 2, crow[...].astype(F32), place)
    place = jnp.where(rows == base + 3, ccol[...].astype(F32), place)
    extra = dot(second_half, place.astype(BF16), NT)

    npred = predt.shape[0]
    kinds = 128
    ind = jnp.where(iota((kinds - npred, obs), 0) == scan[...], 1.0, 0.0)
    basist = jnp.concatenate([predt[...].astype(F32), ind], 0).astype(BF16)
    biast = dot(basist, wbf, NN)
    hi = biast.astype(BF16)
    lo = (biast - hi.astype(F32)).astype(BF16)
    half = chans // 2
    first = base + 4
    er, ec = iota((chans, 128), 0), iota((chans, 128), 1)
    qr, qk = iota((rows_out, kinds), 0), iota((rows_out, kinds), 1)
    for h in range(2):
        mine = (er >= h * half) & (er < (h + 1) * half)
        e = ones_where((ec == er - h * half + first) & mine)
        f = ones_where((ec == er - h * half + first + half) & mine)
        part = (dot(hi, e, NN) + dot(lo, f, NN)).astype(BF16)
        q = qk + h * kinds
        extra = extra + dot(ones_where(qr == (q // CAP) * (2 * CAP) + CAP + q % CAP), part, NN)

    for i in range(steps // 2, steps):
        sums(i)
    rows = acc[...].astype(BF16)
    placed = dot(first_half, rows[:, 0:WIDE], NN) + dot(second_half, rows[:, WIDE:LANES], NN)
    out[:, 0 : WIDE - 128] = placed[:, 0 : WIDE - 128].astype(BF16)
    out[:, WIDE - 128 : WIDE] = (placed[:, WIDE - 128 : WIDE] + extra).astype(BF16)


def picks(slots, offset):
    q, r = iota((slots, 2 * slots), 0), iota((slots, 2 * slots), 1)
    return ones_where(r == (q // CAP) * (2 * CAP) + q % CAP + offset)


def head_kernel(got, head, *, levels, half):
    slots = got.shape[0] // 2
    lanes = got[:, WIDE - 128 : WIDE]
    rest = jnp.transpose(dot(picks(slots, CAP), lanes, NN))
    at = VROWS - 16 - (LANES - 128)
    head[0:16, :] = rest[at : at + 16, :].astype(BF16)
    q, r = iota((8, 2 * slots), 0), iota((8, 2 * slots), 1)
    pick = ones_where(r % (2 * CAP) == q + CAP)
    total = dot(pick, lanes, NN)
    first = levels - (LANES - 128) + 4
    lane = iota((8, 128), 1)
    kept = 128 - first - half
    chunk = jnp.where(lane < half, pltpu.roll(total, 128 - first, 1), 0.0)
    chunk = chunk + jnp.where(lane < kept, pltpu.roll(total, 128 - first - half, 1), 0.0)
    high = chunk.astype(BF16).astype(F32)
    head[16:32, 0:128] = jnp.concatenate([high, chunk - high], 0).astype(BF16)
    head[16:32, 128:slots] = jnp.zeros((16, slots - 128), BF16)


def turn_kernel(got, out):
    slots = got.shape[0] // 2
    out[0:WIDE, :] = jnp.transpose(dot(picks(slots, 0), got[...], NN)).astype(BF16)
    rest = jnp.transpose(dot(picks(slots, CAP), got[...], NN))
    out[WIDE:VROWS, :] = rest[0 : VROWS - WIDE, :].astype(BF16)


def prep_kernel(first_row, h0, h1, h2, h3, colw, roww, lastw, chunk, *, levels):
    heads = (h0, h1, h2, h3)
    part = sum([h[16:32, 0:128].astype(F32) for h in heads])
    four = (part[0:8, :] + part[8:16, :])[0:CAP, :]
    eight = jnp.concatenate([four, four], 0)
    n_rows = chunk.shape[0]
    chunk[...] = jnp.broadcast_to(eight[None], (n_rows // 8, 8, 128)).reshape(n_rows, 128)
    tops = jnp.concatenate([h[0:16, :].astype(F32) for h in heads], 1)
    at = levels - (VROWS - 16)
    fr, cr = tops[at : at + 1, :], tops[at + 2 : at + 3, :]
    n = fr.shape[1]
    turned = jnp.transpose(tops)
    fc, cc = turned[:, at + 1 : at + 2], turned[:, at + 3 : at + 4].astype(jnp.int32)
    cols = iota((n, GC), 1)
    colw[...] = jnp.where(cols == cc, 1.0 - fc, jnp.where(cols == cc + 1, fc, 0.0)).astype(BF16)
    row = cr.astype(jnp.int32)
    rel = iota((BLOCK, n), 0) + first_row[0]
    roww[...] = jnp.where(rel == row, 1.0 - fr, 0.0) + jnp.where(rel == row + 1, fr, 0.0)
    lastw[...] = jnp.broadcast_to(jnp.where(row == GR - 1, fr, 0.0), lastw.shape)


def spill_kernel(a0, a1, a2, a3, colw, lastw, spill):
    part = a0.shape[1]
    out = jnp.zeros((VROWS, GC), F32)
    for j, ref in enumerate((a0, a1, a2, a3)):
        cols = slice(j * part, (j + 1) * part)
        lhs = (ref[...].astype(F32) * lastw[0:1, cols]).astype(BF16)
        out = out + dot(lhs, colw[cols, :], NN)
    spill[...] = out.astype(BF16)


def grid_kernel(a0, a1, a2, a3, colw, roww, out):
    part = a0.shape[1]
    total = jnp.zeros((VCHUNK * BLOCK, GC), F32)
    for j, ref in enumerate((a0, a1, a2, a3)):
        cols = slice(j * part, (j + 1) * part)
        lhs = ref[...].astype(F32)[:, None, :] * roww[:, cols][None, :, :]
        lhs = lhs.reshape(VCHUNK * BLOCK, part).astype(BF16)
        total = total + dot(lhs, colw[cols, :], NN)
    out[...] = total.reshape(VCHUNK, BLOCK, GC)


def join_kernel(grid, spill, out):
    first = iota((VCHUNK, BLOCK, GC), 1) == 0
    out[...] = grid[...] + jnp.where(first, spill[...].astype(F32)[:, None, :], 0.0)


def bias_kernel(got, out, *, half, scale):
    t = jnp.transpose(got[...]) * scale
    n = got.shape[0] // 2
    out[0:half, :] = t[0:half, 0:n]
    out[half : 2 * half, :] = t[0:half, n : 2 * n]


def whole(shape):
    return pl.BlockSpec(shape, lambda *_: (0,) * len(shape))


VM = pl.BlockSpec(memory_space=pltpu.VMEM)
HBM = pl.BlockSpec(memory_space=pltpu.HBM)


def per_device(
    departure, inv_var, k_matrix, frac_row, frac_col, dest_tile, cell_row, cell_col, predictors, scan_pos
):
    n_tile = lax.axis_size("tile")
    n_slot = lax.axis_size("slot")
    obs, chans, levels = k_matrix.shape
    slots = n_tile * CAP
    params = pltpu.CompilerParams(vmem_limit_bytes=VMEM)
    tight = pltpu.CompilerParams(vmem_limit_bytes=56 * 1024 * 1024)
    steps = 10
    flat = lambda x: x.reshape(1, obs)
    small = (
        departure,
        inv_var.reshape(1, chans),
        flat(dest_tile),
        flat(frac_row),
        flat(frac_col),
        flat(cell_row),
        flat(cell_col),
        predictors.T,
        flat(scan_pos),
    )
    send = pl.pallas_call(
        functools.partial(send_kernel, steps=steps),
        out_shape=jax.ShapeDtypeStruct((2 * slots, WIDE), BF16),
        in_specs=[HBM] * (1 + len(small)),
        out_specs=VM,
        scratch_shapes=[pltpu.VMEM(x.shape, x.dtype) for x in small]
        + [
            pltpu.VMEM((chans, obs, levels), BF16),
            pltpu.VMEM((obs, LANES), F32),
            pltpu.SemaphoreType.DMA((steps,)),
            pltpu.SemaphoreType.DMA((len(small),)),
        ],
        compiler_params=tight,
        name="send",
    )(jnp.transpose(k_matrix, (1, 0, 2)), *small)
    got = lax.all_to_all(send.reshape(n_tile, 2 * CAP, WIDE), "tile", 0, 0, tiled=True).reshape(2 * slots, WIDE)
    head = pl.pallas_call(
        functools.partial(head_kernel, levels=levels, half=chans // 2),
        out_shape=jax.ShapeDtypeStruct((32, slots), BF16),
        in_specs=[VM],
        out_specs=VM,
        compiler_params=params,
        name="head",
    )(got)
    turned = pl.pallas_call(
        turn_kernel,
        out_shape=jax.ShapeDtypeStruct((VROWS, slots), BF16),
        in_specs=[VM],
        out_specs=VM,
        compiler_params=params,
        name="turn",
    )(got)

    def around(x):
        return [x] + [lax.ppermute(x, "slot", [(i, (i + d) % n_slot) for i in range(n_slot)]) for d in (1, 3, 2)]

    turned, *heads = lax.optimization_barrier((turned, *around(head)))
    blocks = around(turned)
    total = n_slot * slots
    first_row = (lax.axis_index("slot") * BLOCK).astype(jnp.int32).reshape(1)
    colw, roww, lastw, chunk = pl.pallas_call(
        functools.partial(prep_kernel, levels=levels),
        out_shape=(
            jax.ShapeDtypeStruct((total, GC), BF16),
            jax.ShapeDtypeStruct((BLOCK, total), F32),
            jax.ShapeDtypeStruct((8, total), F32),
            jax.ShapeDtypeStruct((slots, 128), F32),
        ),
        in_specs=[pl.BlockSpec(memory_space=pltpu.SMEM)] + [VM] * 4,
        out_specs=(VM,) * 4,
        compiler_params=params,
        name="prep",
    )(first_row, *heads)
    chunks = lax.all_to_all(chunk.reshape(n_tile, CAP, 128), "tile", 0, 0, tiled=True).reshape(slots, 128)
    spill = pl.pallas_call(
        spill_kernel,
        out_shape=jax.ShapeDtypeStruct((VROWS, GC), BF16),
        in_specs=[VM] * 6,
        out_specs=VM,
        compiler_params=params,
        name="spill",
    )(*blocks, colw, lastw)
    pairs = [(t * n_slot, ((t + 1) % n_tile) * n_slot) for t in range(n_tile)]
    arrived = lax.ppermute(spill, ("tile", "slot"), pairs)
    level_block = pl.BlockSpec((VCHUNK, BLOCK, GC), lambda i: (i, 0, 0))
    own = pl.pallas_call(
        grid_kernel,
        grid=(VROWS // VCHUNK,),
        out_shape=jax.ShapeDtypeStruct((VROWS, BLOCK, GC), F32),
        in_specs=[pl.BlockSpec((VCHUNK, slots), lambda i: (i, 0))] * 4 + [whole((total, GC)), whole((BLOCK, total))],
        out_specs=level_block,
        compiler_params=params,
        name="grid",
    )(*blocks, colw, roww)
    grid = pl.pallas_call(
        join_kernel,
        grid=(VROWS // VCHUNK,),
        out_shape=jax.ShapeDtypeStruct((levels, BLOCK, GC), F32),
        in_specs=[level_block, pl.BlockSpec((VCHUNK, GC), lambda i: (i, 0))],
        out_specs=level_block,
        compiler_params=params,
        name="join",
    )(own, arrived)
    chunks, grid = lax.optimization_barrier((chunks, grid))
    bias = pl.pallas_call(
        functools.partial(bias_kernel, half=chans // 2, scale=1.0 / math.sqrt(obs * n_tile * n_slot)),
        out_shape=jax.ShapeDtypeStruct((chans, 128), F32),
        in_specs=[VM],
        out_specs=VM,
        compiler_params=params,
        name="bias",
    )(chunks)
    return jnp.transpose(grid, (1, 2, 0)), bias


def solution(mesh):
    both = ("tile", "slot")
    placed = (
        P(both, None),
        P(),
        P(both, None, None),
        P(both),
        P(both),
        P(both, None),
        P(both),
        P(both),
        P(both, None),
        P(both),
    )
    return jax.shard_map(
        per_device,
        mesh=mesh,
        in_specs=placed,
        out_specs=(P(both, None, None), P()),
        check_vma=False,
    )
```

```python
import functools
import math

import jax
import jax.numpy as jnp
from jax import lax
from jax.experimental import pallas as pl
from jax.experimental.pallas import tpu as pltpu
from jax.sharding import PartitionSpec as P

F32 = jnp.float32
BF16 = jnp.bfloat16
NT = (((1,), (1,)), ((), ()))
NN = (((1,), (0,)), ((), ()))

CAP = 4
GR = 32
GC = 256
LANES = 512
WIDE = LANES // 2
VROWS = 416
PARTS = ((0, 112), (112, 224), (224, 320), (320, 416))
BLOCK = 8
VMEM = 24 * 1024 * 1024


def iota(shape, dim):
    return lax.broadcasted_iota(jnp.int32, shape, dim)


def dot(a, b, dims):
    return lax.dot_general(a, b, dims, preferred_element_type=F32)


def ones_where(mask):
    return jnp.where(mask, 1.0, 0.0).astype(BF16)


def send_kernel(*refs, steps):
    k_hbm, small_hbm, out, small, kbuf, acc, sems, small_sems = refs[0], refs[1:10], *refs[10:11], refs[11:20], *refs[20:]
    chans, obs, levels = k_hbm.shape
    per = chans // steps
    small_copies = [
        pltpu.make_async_copy(src, dst, small_sems.at[i]) for i, (src, dst) in enumerate(zip(small_hbm, small))
    ]
    copies = [
        pltpu.make_async_copy(k_hbm.at[pl.ds(i * per, per)], kbuf.at[pl.ds(i * per, per)], sems.at[i])
        for i in range(steps)
    ]
    for copy in small_copies[:2] + copies[:2] + small_copies[2:] + copies[2:]:
        copy.start()
    dep, inv, tile, frow, fcol, crow, ccol, predt, scan = small
    rows_out = out.shape[0]

    kinds = 128
    half = chans // 2
    base = levels - (LANES - 128)
    first = base + 4
    er, ec = iota((chans, 128), 0), iota((chans, 128), 1)
    qr, qk = iota((rows_out, kinds), 0), iota((rows_out, kinds), 1)
    spreads, places = [], []
    for h in range(2):
        mine = (er >= h * half) & (er < (h + 1) * half)
        e = ones_where((ec == er - h * half + first) & mine)
        f = ones_where((ec == er - h * half + first + half) & mine)
        spreads.append((e, f))
        q = qk + h * kinds
        places.append(ones_where(qr == (q // CAP) * (2 * CAP) + CAP + q % CAP))
    acc[...] = jnp.zeros(acc.shape, F32)
    for copy in small_copies[:2]:
        copy.wait()
    wbf = (dep[...].astype(F32) * inv[...]).astype(BF16)
    w = wbf.astype(F32)

    def sums(i):
        copies[i].wait()
        for r in range(0, obs, 16):
            total = acc[r : r + 16, 0:levels]
            for c in range(i * per, (i + 1) * per):
                total = total + w[r : r + 16, c : c + 1] * kbuf[c, r : r + 16, :].astype(F32)
            acc[r : r + 16, 0:levels] = total

    for i in range(steps // 2):
        sums(i)
    for copy in small_copies[2:]:
        copy.wait()

    tr = jnp.broadcast_to(tile[...].astype(F32), (obs, obs))
    ri, ci = iota((obs, obs), 0), iota((obs, obs), 1)
    tc = jnp.sum(jnp.where(ri == ci, tr, 0.0), 1, keepdims=True)
    rank = jnp.sum(jnp.where((tc == tr) & (ri < ci), 1.0, 0.0), 0, keepdims=True)
    slot = (tile[...].astype(F32) * (2 * CAP) + rank).astype(jnp.int32)
    at = iota((rows_out, obs), 0)
    first_half, second_half = ones_where(at == slot), ones_where(at == slot + CAP)

    rows = iota((128, obs), 0)
    place = jnp.where(rows == base, frow[...].astype(F32), 0.0)
    place = jnp.where(rows == base + 1, fcol[...].astype(F32), place)
    place = jnp.where(rows == base + 2, crow[...].astype(F32), place)
    place = jnp.where(rows == base + 3, ccol[...].astype(F32), place)
    extra = dot(second_half, place.astype(BF16), NT)

    npred = predt.shape[0]
    ind = jnp.where(iota((kinds - npred, obs), 0) == scan[...], 1.0, 0.0)
    basist = jnp.concatenate([predt[...].astype(F32), ind], 0).astype(BF16)
    biast = dot(basist, wbf, NN)
    hi = biast.astype(BF16)
    lo = (biast - hi.astype(F32)).astype(BF16)
    for (e, f), place in zip(spreads, places):
        part = (dot(hi, e, NN) + dot(lo, f, NN)).astype(BF16)
        extra = extra + dot(place, part, NN)

    for i in range(steps // 2, steps):
        sums(i)
    rows = acc[...].astype(BF16)
    placed = dot(first_half, rows[:, 0:WIDE], NN) + dot(second_half, rows[:, WIDE:LANES], NN)
    out[:, 0 : WIDE - 128] = placed[:, 0 : WIDE - 128].astype(BF16)
    out[:, WIDE - 128 : WIDE] = (placed[:, WIDE - 128 : WIDE] + extra).astype(BF16)


def picks(slots, offset):
    q, r = iota((slots, 2 * slots), 0), iota((slots, 2 * slots), 1)
    return ones_where(r == (q // CAP) * (2 * CAP) + q % CAP + offset)


def head_kernel(got, head, *, levels, half):
    slots = got.shape[0] // 2
    lanes = got[:, WIDE - 128 : WIDE]
    rest = jnp.transpose(dot(picks(slots, CAP), lanes, NN))
    at = VROWS - 16 - (LANES - 128)
    head[0:16, :] = rest[at : at + 16, :].astype(BF16)
    q, r = iota((8, 2 * slots), 0), iota((8, 2 * slots), 1)
    pick = ones_where(r % (2 * CAP) == q + CAP)
    total = dot(pick, lanes, NN)
    first = levels - (LANES - 128) + 4
    lane = iota((8, 128), 1)
    kept = 128 - first - half
    chunk = jnp.where(lane < half, pltpu.roll(total, 128 - first, 1), 0.0)
    chunk = chunk + jnp.where(lane < kept, pltpu.roll(total, 128 - first - half, 1), 0.0)
    high = chunk.astype(BF16).astype(F32)
    head[16:32, 0:128] = jnp.concatenate([high, chunk - high], 0).astype(BF16)
    head[16:32, 128:slots] = jnp.zeros((16, slots - 128), BF16)


def turn_kernel(got, head, out):
    slots = got.shape[0] // 2
    out[0:WIDE, :] = jnp.transpose(dot(picks(slots, 0), got[...], NN)).astype(BF16)
    rest = jnp.transpose(dot(picks(slots, CAP), got[...], NN))
    out[WIDE : VROWS - 16, :] = rest[0 : VROWS - 16 - WIDE, :].astype(BF16)
    out[VROWS - 16 : VROWS, :] = head[0:16, :]


def prep_kernel(first_row, h0, h1, h2, h3, colw, roww, lastw, chunk, *, levels):
    heads = (h0, h1, h2, h3)
    part = sum([h[16:32, 0:128].astype(F32) for h in heads])
    four = (part[0:8, :] + part[8:16, :])[0:CAP, :]
    eight = jnp.concatenate([four, four], 0)
    n_rows = chunk.shape[0]
    chunk[...] = jnp.broadcast_to(eight[None], (n_rows // 8, 8, 128)).reshape(n_rows, 128)
    tops = jnp.concatenate([h[0:16, :].astype(F32) for h in heads], 1)
    at = levels - (VROWS - 16)
    fr, cr = tops[at : at + 1, :], tops[at + 2 : at + 3, :]
    n = fr.shape[1]
    turned = jnp.transpose(tops)
    fc, cc = turned[:, at + 1 : at + 2], turned[:, at + 3 : at + 4].astype(jnp.int32)
    cols = iota((n, GC), 1)
    colw[...] = jnp.where(cols == cc, 1.0 - fc, jnp.where(cols == cc + 1, fc, 0.0)).astype(BF16)
    row = cr.astype(jnp.int32)
    rel = iota((BLOCK, n), 0) + first_row[0]
    roww[...] = jnp.where(rel == row, 1.0 - fr, 0.0) + jnp.where(rel == row + 1, fr, 0.0)
    lastw[...] = jnp.broadcast_to(jnp.where(row == GR - 1, fr, 0.0), lastw.shape)


def spill_kernel(a0, a1, a2, a3, colw, lastw, *spills):
    part = a0.shape[1]
    out = jnp.zeros((VROWS, GC), F32)
    for j, ref in enumerate((a0, a1, a2, a3)):
        cols = slice(j * part, (j + 1) * part)
        lhs = (ref[...].astype(F32) * lastw[0:1, cols]).astype(BF16)
        out = out + dot(lhs, colw[cols, :], NN)
    for spill, (lo, hi) in zip(spills, PARTS):
        spill[...] = out[lo:hi, :].astype(BF16)


def grid_kernel(a0, a1, a2, a3, colw, roww, out):
    part = a0.shape[1]
    for lo, hi in PARTS:
        total = jnp.zeros(((hi - lo) * BLOCK, GC), F32)
        for j, ref in enumerate((a0, a1, a2, a3)):
            cols = slice(j * part, (j + 1) * part)
            lhs = ref[lo:hi, :].astype(F32)[:, None, :] * roww[:, cols][None, :, :]
            lhs = lhs.reshape((hi - lo) * BLOCK, part).astype(BF16)
            total = total + dot(lhs, colw[cols, :], NN)
        out[lo:hi] = total.reshape(hi - lo, BLOCK, GC)


def join_kernel(grid, *refs):
    spills, out, joined, sems = refs[0 : len(PARTS)], *refs[len(PARTS) :]
    levels = out.shape[0]
    copies = []
    for i, (lo, hi) in enumerate(PARTS):
        first = iota((hi - lo, BLOCK, GC), 1) == 0
        joined[lo:hi] = grid[lo:hi] + jnp.where(first, spills[i][...].astype(F32)[:, None, :], 0.0)
        size = min(hi, levels) - lo
        copies.append(pltpu.make_async_copy(joined.at[pl.ds(lo, size)], out.at[pl.ds(lo, size)], sems.at[i]))
        copies[i].start()
    for copy in copies:
        copy.wait()


def bias_kernel(got, out, *, half, scale):
    t = jnp.transpose(got[...]) * scale
    n = got.shape[0] // 2
    out[0:half, :] = t[0:half, 0:n]
    out[half : 2 * half, :] = t[0:half, n : 2 * n]


VM = pl.BlockSpec(memory_space=pltpu.VMEM)
HBM = pl.BlockSpec(memory_space=pltpu.HBM)


def per_device(
    departure, inv_var, k_matrix, frac_row, frac_col, dest_tile, cell_row, cell_col, predictors, scan_pos
):
    n_tile = lax.axis_size("tile")
    n_slot = lax.axis_size("slot")
    obs, chans, levels = k_matrix.shape
    slots = n_tile * CAP
    params = pltpu.CompilerParams(vmem_limit_bytes=VMEM)
    tight = pltpu.CompilerParams(vmem_limit_bytes=56 * 1024 * 1024)
    steps = 10
    flat = lambda x: x.reshape(1, obs)
    small = (
        departure,
        inv_var.reshape(1, chans),
        flat(dest_tile),
        flat(frac_row),
        flat(frac_col),
        flat(cell_row),
        flat(cell_col),
        predictors.T,
        flat(scan_pos),
    )
    send = pl.pallas_call(
        functools.partial(send_kernel, steps=steps),
        out_shape=jax.ShapeDtypeStruct((2 * slots, WIDE), BF16),
        in_specs=[HBM] * (1 + len(small)),
        out_specs=VM,
        scratch_shapes=[pltpu.VMEM(x.shape, x.dtype) for x in small]
        + [
            pltpu.VMEM((chans, obs, levels), BF16),
            pltpu.VMEM((obs, LANES), F32),
            pltpu.SemaphoreType.DMA((steps,)),
            pltpu.SemaphoreType.DMA((len(small),)),
        ],
        compiler_params=tight,
        name="send",
    )(jnp.transpose(k_matrix, (1, 0, 2)), *small)
    got = lax.all_to_all(send.reshape(n_tile, 2 * CAP, WIDE), "tile", 0, 0, tiled=True).reshape(2 * slots, WIDE)
    head = pl.pallas_call(
        functools.partial(head_kernel, levels=levels, half=chans // 2),
        out_shape=jax.ShapeDtypeStruct((32, slots), BF16),
        in_specs=[VM],
        out_specs=VM,
        compiler_params=params,
        name="head",
    )(got)
    turned = pl.pallas_call(
        turn_kernel,
        out_shape=jax.ShapeDtypeStruct((VROWS, slots), BF16),
        in_specs=[VM, VM],
        out_specs=VM,
        compiler_params=params,
        cost_estimate=pl.CostEstimate(flops=2**30, bytes_accessed=2**22, transcendentals=0),
        name="turn",
    )(got, head)

    def around(x):
        return [x] + [lax.ppermute(x, "slot", [(i, (i + d) % n_slot) for i in range(n_slot)]) for d in (1, 3, 2)]

    heads = around(head)
    blocks = around(turned)
    total = n_slot * slots
    first_row = (lax.axis_index("slot") * BLOCK).astype(jnp.int32).reshape(1)
    colw, roww, lastw, chunk = pl.pallas_call(
        functools.partial(prep_kernel, levels=levels),
        out_shape=(
            jax.ShapeDtypeStruct((total, GC), BF16),
            jax.ShapeDtypeStruct((BLOCK, total), F32),
            jax.ShapeDtypeStruct((8, total), F32),
            jax.ShapeDtypeStruct((slots, 128), F32),
        ),
        in_specs=[pl.BlockSpec(memory_space=pltpu.SMEM)] + [VM] * 4,
        out_specs=(VM,) * 4,
        compiler_params=params,
        cost_estimate=pl.CostEstimate(flops=10**11, bytes_accessed=10**8, transcendentals=0),
        name="prep",
    )(first_row, *heads)
    chunks = lax.all_to_all(chunk.reshape(n_tile, CAP, 128), "tile", 0, 0, tiled=True).reshape(slots, 128)
    spills = pl.pallas_call(
        spill_kernel,
        out_shape=tuple(jax.ShapeDtypeStruct((hi - lo, GC), BF16) for lo, hi in PARTS),
        in_specs=[VM] * 6,
        out_specs=(VM,) * len(PARTS),
        compiler_params=params,
        name="spill",
    )(*blocks, colw, lastw)
    arrived = [
        lax.ppermute(
            x, ("tile", "slot"), [(t * n_slot + q % n_slot, ((t + 1) % n_tile) * n_slot) for t in range(n_tile)]
        )
        for q, x in enumerate(spills)
    ]
    own = pl.pallas_call(
        grid_kernel,
        out_shape=jax.ShapeDtypeStruct((VROWS, BLOCK, GC), F32),
        in_specs=[VM] * 6,
        out_specs=VM,
        compiler_params=params,
        name="grid",
    )(*blocks, colw, roww)
    grid = pl.pallas_call(
        join_kernel,
        out_shape=jax.ShapeDtypeStruct((levels, BLOCK, GC), F32),
        in_specs=[VM] * (1 + len(PARTS)),
        out_specs=HBM,
        scratch_shapes=[pltpu.VMEM((VROWS, BLOCK, GC), F32), pltpu.SemaphoreType.DMA((len(PARTS),))],
        compiler_params=params,
        name="join",
    )(own, *arrived)
    chunks, grid = lax.optimization_barrier((chunks, grid))
    bias = pl.pallas_call(
        functools.partial(bias_kernel, half=chans // 2, scale=1.0 / math.sqrt(obs * n_tile * n_slot)),
        out_shape=jax.ShapeDtypeStruct((chans, 128), F32),
        in_specs=[VM],
        out_specs=VM,
        compiler_params=params,
        name="bias",
    )(chunks)
    return jnp.transpose(grid, (1, 2, 0)), bias


def solution(mesh):
    both = ("tile", "slot")
    placed = (
        P(both, None),
        P(),
        P(both, None, None),
        P(both),
        P(both),
        P(both, None),
        P(both),
        P(both),
        P(both, None),
        P(both),
    )
    return jax.shard_map(
        per_device,
        mesh=mesh,
        in_specs=placed,
        out_specs=(P(both, None, None), P()),
        check_vma=False,
    )
```

```python
import functools
import math

import jax
import jax.numpy as jnp
from jax import lax
from jax.experimental import pallas as pl
from jax.experimental.pallas import tpu as pltpu
from jax.sharding import PartitionSpec as P

F32 = jnp.float32
BF16 = jnp.bfloat16
NT = (((1,), (1,)), ((), ()))
NN = (((1,), (0,)), ((), ()))

CAP = 4
GR = 32
GC = 256
LANES = 512
WIDE = LANES // 2
VROWS = 416
PARTS = ((0, 112), (112, 224), (224, 320), (320, 416))
BLOCK = 8
VMEM = 24 * 1024 * 1024


def iota(shape, dim):
    return lax.broadcasted_iota(jnp.int32, shape, dim)


def dot(a, b, dims):
    return lax.dot_general(a, b, dims, preferred_element_type=F32)


def ones_where(mask):
    return jnp.where(mask, 1.0, 0.0).astype(BF16)


def send_kernel(*refs, steps):
    k_hbm, small_hbm, out, small, kbuf, acc, sems, small_sems = refs[0], refs[1:10], *refs[10:11], refs[11:20], *refs[20:]
    chans, obs, levels = k_hbm.shape
    per = chans // steps
    small_copies = [
        pltpu.make_async_copy(src, dst, small_sems.at[i]) for i, (src, dst) in enumerate(zip(small_hbm, small))
    ]
    copies = [
        pltpu.make_async_copy(k_hbm.at[pl.ds(i * per, per)], kbuf.at[pl.ds(i * per, per)], sems.at[i])
        for i in range(steps)
    ]
    for copy in small_copies[:2] + copies[:2] + small_copies[2:] + copies[2:]:
        copy.start()
    dep, inv, tile, frow, fcol, crow, ccol, predt, scan = small
    rows_out = out.shape[0]

    kinds = 128
    half = chans // 2
    base = levels - (LANES - 128)
    first = base + 4
    er, ec = iota((chans, 128), 0), iota((chans, 128), 1)
    qr, qk = iota((rows_out, kinds), 0), iota((rows_out, kinds), 1)
    spreads, places = [], []
    for h in range(2):
        mine = (er >= h * half) & (er < (h + 1) * half)
        e = ones_where((ec == er - h * half + first) & mine)
        f = ones_where((ec == er - h * half + first + half) & mine)
        spreads.append((e, f))
        q = qk + h * kinds
        places.append(ones_where(qr == (q // CAP) * (2 * CAP) + CAP + q % CAP))
    acc[...] = jnp.zeros(acc.shape, F32)
    for copy in small_copies[:2]:
        copy.wait()
    wbf = (dep[...].astype(F32) * inv[...]).astype(BF16)
    w = wbf.astype(F32)

    def sums(i):
        copies[i].wait()
        for r in range(0, obs, 16):
            total = acc[r : r + 16, 0:levels]
            for c in range(i * per, (i + 1) * per):
                total = total + w[r : r + 16, c : c + 1] * kbuf[c, r : r + 16, :].astype(F32)
            acc[r : r + 16, 0:levels] = total

    for i in range(steps // 2):
        sums(i)
    for copy in small_copies[2:]:
        copy.wait()

    tr = jnp.broadcast_to(tile[...].astype(F32), (obs, obs))
    ri, ci = iota((obs, obs), 0), iota((obs, obs), 1)
    tc = jnp.sum(jnp.where(ri == ci, tr, 0.0), 1, keepdims=True)
    rank = jnp.sum(jnp.where((tc == tr) & (ri < ci), 1.0, 0.0), 0, keepdims=True)
    slot = (tile[...].astype(F32) * (2 * CAP) + rank).astype(jnp.int32)
    at = iota((rows_out, obs), 0)
    first_half, second_half = ones_where(at == slot), ones_where(at == slot + CAP)

    rows = iota((128, obs), 0)
    place = jnp.where(rows == base, frow[...].astype(F32), 0.0)
    place = jnp.where(rows == base + 1, fcol[...].astype(F32), place)
    place = jnp.where(rows == base + 2, crow[...].astype(F32), place)
    place = jnp.where(rows == base + 3, ccol[...].astype(F32), place)
    extra = dot(second_half, place.astype(BF16), NT)

    npred = predt.shape[0]
    ind = jnp.where(iota((kinds - npred, obs), 0) == scan[...], 1.0, 0.0)
    basist = jnp.concatenate([predt[...].astype(F32), ind], 0).astype(BF16)
    biast = dot(basist, wbf, NN)
    hi = biast.astype(BF16)
    lo = (biast - hi.astype(F32)).astype(BF16)
    for (e, f), place in zip(spreads, places):
        part = (dot(hi, e, NN) + dot(lo, f, NN)).astype(BF16)
        extra = extra + dot(place, part, NN)

    for i in range(steps // 2, steps):
        sums(i)
    rows = acc[...].astype(BF16)
    placed = dot(first_half, rows[:, 0:WIDE], NN) + dot(second_half, rows[:, WIDE:LANES], NN)
    out[:, 0 : WIDE - 128] = placed[:, 0 : WIDE - 128].astype(BF16)
    out[:, WIDE - 128 : WIDE] = (placed[:, WIDE - 128 : WIDE] + extra).astype(BF16)


def picks(slots, offset):
    q, r = iota((slots, 2 * slots), 0), iota((slots, 2 * slots), 1)
    return ones_where(r == (q // CAP) * (2 * CAP) + q % CAP + offset)


def chunk_kernel(got, chunk, *, levels, half):
    slots = got.shape[0] // 2
    q, r = iota((slots, 2 * slots), 0), iota((slots, 2 * slots), 1)
    pick = ones_where(r % (2 * CAP) == q % CAP + CAP)
    total = dot(pick, got[:, WIDE - 128 : WIDE], NN)
    first = levels - (LANES - 128) + 4
    lane = iota((slots, 128), 1)
    kept = 128 - first - half
    sums = jnp.where(lane < half, pltpu.roll(total, 128 - first, 1), 0.0)
    chunk[...] = sums + jnp.where(lane < kept, pltpu.roll(total, 128 - first - half, 1), 0.0)


def turn_kernel(got, out):
    slots = got.shape[0] // 2
    out[0:WIDE, :] = jnp.transpose(dot(picks(slots, 0), got[...], NN)).astype(BF16)
    rest = jnp.transpose(dot(picks(slots, CAP), got[...], NN))
    out[WIDE:VROWS, :] = rest[0 : VROWS - WIDE, :].astype(BF16)


def prep_kernel(first_row, a0, a1, a2, a3, spill, colw, roww, *, levels):
    refs = (a0, a1, a2, a3)
    tops = jnp.concatenate([ref[VROWS - 16 : VROWS, :].astype(F32) for ref in refs], 1)
    at = levels - (VROWS - 16)
    fr, fc = tops[at : at + 1, :], tops[at + 1 : at + 2, :]
    row, col = tops[at + 2 : at + 3, :].astype(jnp.int32), tops[at + 3 : at + 4, :].astype(jnp.int32)
    n = fr.shape[1]
    cols = iota((GC, n), 0)
    cw = jnp.where(cols == col, 1.0 - fc, jnp.where(cols == col + 1, fc, 0.0)).astype(BF16)
    colw[...] = cw
    rel = iota((BLOCK, n), 0) + first_row[0]
    roww[...] = jnp.where(rel == row, 1.0 - fr, 0.0) + jnp.where(rel == row + 1, fr, 0.0)
    last = jnp.where(row == GR - 1, fr, 0.0)
    part = a0.shape[1]
    out = jnp.zeros((VROWS, GC), F32)
    for j, ref in enumerate(refs):
        cols = slice(j * part, (j + 1) * part)
        lhs = (ref[...].astype(F32) * last[:, cols]).astype(BF16)
        out = out + dot(lhs, cw[:, cols], NT)
    spill[...] = out.astype(BF16)


def grid_kernel(a0, a1, a2, a3, colw, roww, out):
    part = a0.shape[1]
    for lo, hi in PARTS:
        total = jnp.zeros(((hi - lo) * BLOCK, GC), F32)
        for j, ref in enumerate((a0, a1, a2, a3)):
            cols = slice(j * part, (j + 1) * part)
            lhs = ref[lo:hi, :].astype(F32)[:, None, :] * roww[:, cols][None, :, :]
            lhs = lhs.reshape((hi - lo) * BLOCK, part).astype(BF16)
            total = total + dot(lhs, colw[:, cols], NT)
        out[lo:hi] = total.reshape(hi - lo, BLOCK, GC)


def join_kernel(grid, spill, out, joined, sems):
    levels = out.shape[0]
    copies = []
    for i, (lo, hi) in enumerate(PARTS):
        first = iota((hi - lo, BLOCK, GC), 1) == 0
        joined[lo:hi] = grid[lo:hi] + jnp.where(first, spill[lo:hi, :].astype(F32)[:, None, :], 0.0)
        size = min(hi, levels) - lo
        copies.append(pltpu.make_async_copy(joined.at[pl.ds(lo, size)], out.at[pl.ds(lo, size)], sems.at[i]))
        copies[i].start()
    for copy in copies:
        copy.wait()


def slot_bias_kernel(got, out, *, half):
    t = jnp.transpose(got[...])
    n = got.shape[0] // 2
    out[0:half, :] = t[0:half, 0:n]
    out[half : 2 * half, :] = t[0:half, n : 2 * n]


def bias_kernel(b0, b1, b2, b3, out, *, scale):
    out[...] = ((b0[...] + b1[...]) + (b2[...] + b3[...])) * scale


VM = pl.BlockSpec(memory_space=pltpu.VMEM)
HBM = pl.BlockSpec(memory_space=pltpu.HBM)


def per_device(
    departure, inv_var, k_matrix, frac_row, frac_col, dest_tile, cell_row, cell_col, predictors, scan_pos
):
    n_tile = lax.axis_size("tile")
    n_slot = lax.axis_size("slot")
    obs, chans, levels = k_matrix.shape
    slots = n_tile * CAP
    params = pltpu.CompilerParams(vmem_limit_bytes=VMEM)
    tight = pltpu.CompilerParams(vmem_limit_bytes=56 * 1024 * 1024)
    steps = 10
    flat = lambda x: x.reshape(1, obs)
    small = (
        departure,
        inv_var.reshape(1, chans),
        flat(dest_tile),
        flat(frac_row),
        flat(frac_col),
        flat(cell_row),
        flat(cell_col),
        predictors.T,
        flat(scan_pos),
    )
    send = pl.pallas_call(
        functools.partial(send_kernel, steps=steps),
        out_shape=jax.ShapeDtypeStruct((2 * slots, WIDE), BF16),
        in_specs=[HBM] * (1 + len(small)),
        out_specs=VM,
        scratch_shapes=[pltpu.VMEM(x.shape, x.dtype) for x in small]
        + [
            pltpu.VMEM((chans, obs, levels), BF16),
            pltpu.VMEM((obs, LANES), F32),
            pltpu.SemaphoreType.DMA((steps,)),
            pltpu.SemaphoreType.DMA((len(small),)),
        ],
        compiler_params=tight,
        name="send",
    )(jnp.transpose(k_matrix, (1, 0, 2)), *small)
    got = lax.all_to_all(send.reshape(n_tile, 2 * CAP, WIDE), "tile", 0, 0, tiled=True).reshape(2 * slots, WIDE)
    turned = pl.pallas_call(
        turn_kernel,
        out_shape=jax.ShapeDtypeStruct((VROWS, slots), BF16),
        in_specs=[VM],
        out_specs=VM,
        compiler_params=params,
        name="turn",
    )(got)

    def around(x):
        return [x] + [lax.ppermute(x, "slot", [(i, (i + d) % n_slot) for i in range(n_slot)]) for d in (1, 3, 2)]

    blocks = around(turned)
    chunk = pl.pallas_call(
        functools.partial(chunk_kernel, levels=levels, half=chans // 2),
        out_shape=jax.ShapeDtypeStruct((slots, 128), F32),
        in_specs=[VM],
        out_specs=VM,
        compiler_params=params,
        name="chunk",
    )(got)
    chunks = lax.all_to_all(chunk.reshape(n_tile, CAP, 128), "tile", 0, 0, tiled=True).reshape(slots, 128)
    total = n_slot * slots
    first_row = (lax.axis_index("slot") * BLOCK).astype(jnp.int32).reshape(1)
    spill, colw, roww = pl.pallas_call(
        functools.partial(prep_kernel, levels=levels),
        out_shape=(
            jax.ShapeDtypeStruct((VROWS, GC), BF16),
            jax.ShapeDtypeStruct((GC, total), BF16),
            jax.ShapeDtypeStruct((BLOCK, total), F32),
        ),
        in_specs=[pl.BlockSpec(memory_space=pltpu.SMEM)] + [VM] * 4,
        out_specs=(VM,) * 3,
        compiler_params=params,
        name="prep",
    )(first_row, *blocks)
    pairs = [(t * n_slot, ((t + 1) % n_tile) * n_slot) for t in range(n_tile)]
    arrived = lax.ppermute(spill, ("tile", "slot"), pairs)
    own = pl.pallas_call(
        grid_kernel,
        out_shape=jax.ShapeDtypeStruct((VROWS, BLOCK, GC), F32),
        in_specs=[VM] * 6,
        out_specs=VM,
        compiler_params=params,
        name="grid",
    )(*blocks, colw, roww)
    slot_bias = pl.pallas_call(
        functools.partial(slot_bias_kernel, half=chans // 2),
        out_shape=jax.ShapeDtypeStruct((chans, 128), F32),
        in_specs=[VM],
        out_specs=VM,
        compiler_params=params,
        name="slot_bias",
    )(chunks)
    biases = around(slot_bias)
    grid = pl.pallas_call(
        join_kernel,
        out_shape=jax.ShapeDtypeStruct((levels, BLOCK, GC), F32),
        in_specs=[VM] * 2,
        out_specs=HBM,
        scratch_shapes=[pltpu.VMEM((VROWS, BLOCK, GC), F32), pltpu.SemaphoreType.DMA((len(PARTS),))],
        compiler_params=params,
        name="join",
    )(own, arrived)
    *biases, grid = lax.optimization_barrier((*biases, grid))
    bias = pl.pallas_call(
        functools.partial(bias_kernel, scale=1.0 / math.sqrt(obs * n_tile * n_slot)),
        out_shape=jax.ShapeDtypeStruct((chans, 128), F32),
        in_specs=[VM] * 4,
        out_specs=VM,
        compiler_params=params,
        name="bias",
    )(*biases)
    return jnp.transpose(grid, (1, 2, 0)), bias


def solution(mesh):
    both = ("tile", "slot")
    placed = (
        P(both, None),
        P(),
        P(both, None, None),
        P(both),
        P(both),
        P(both, None),
        P(both),
        P(both),
        P(both, None),
        P(both),
    )
    return jax.shard_map(
        per_device,
        mesh=mesh,
        in_specs=placed,
        out_specs=(P(both, None, None), P()),
        check_vma=False,
    )
```

```python
import functools
import math

import jax
import jax.numpy as jnp
from jax import lax
from jax.experimental import pallas as pl
from jax.experimental.pallas import tpu as pltpu
from jax.sharding import PartitionSpec as P

F32 = jnp.float32
BF16 = jnp.bfloat16
NT = (((1,), (1,)), ((), ()))
NN = (((1,), (0,)), ((), ()))

CAP = 4
GR = 32
GC = 256
LANES = 512
WIDE = LANES // 2
VROWS = 416
PARTS = ((0, 112), (112, 224), (224, 320), (320, 416))
BLOCK = 8
VMEM = 24 * 1024 * 1024


def iota(shape, dim):
    return lax.broadcasted_iota(jnp.int32, shape, dim)


def dot(a, b, dims):
    return lax.dot_general(a, b, dims, preferred_element_type=F32)


def ones_where(mask):
    return jnp.where(mask, 1.0, 0.0).astype(BF16)


def send_kernel(*refs, steps):
    k_hbm, small_hbm, out, small, kbuf, acc, sems, small_sems = refs[0], refs[1:10], *refs[10:11], refs[11:20], *refs[20:]
    chans, obs, levels = k_hbm.shape
    per = chans // steps
    small_copies = [
        pltpu.make_async_copy(src, dst, small_sems.at[i]) for i, (src, dst) in enumerate(zip(small_hbm, small))
    ]
    copies = [
        pltpu.make_async_copy(k_hbm.at[pl.ds(i * per, per)], kbuf.at[pl.ds(i * per, per)], sems.at[i])
        for i in range(steps)
    ]
    for copy in small_copies[:2] + copies[:2] + small_copies[2:] + copies[2:]:
        copy.start()
    dep, inv, tile, frow, fcol, crow, ccol, predt, scan = small
    rows_out = out.shape[0]

    kinds = 128
    half = chans // 2
    base = levels - (LANES - 128)
    first = base + 4
    er, ec = iota((chans, 128), 0), iota((chans, 128), 1)
    qr, qk = iota((rows_out, kinds), 0), iota((rows_out, kinds), 1)
    spreads, places = [], []
    for h in range(2):
        mine = (er >= h * half) & (er < (h + 1) * half)
        e = ones_where((ec == er - h * half + first) & mine)
        f = ones_where((ec == er - h * half + first + half) & mine)
        spreads.append((e, f))
        q = qk + h * kinds
        places.append(ones_where(qr == (q // CAP) * (2 * CAP) + CAP + q % CAP))
    acc[...] = jnp.zeros(acc.shape, F32)
    for copy in small_copies[:2]:
        copy.wait()
    wbf = (dep[...].astype(F32) * inv[...]).astype(BF16)
    w = wbf.astype(F32)

    def sums(i):
        copies[i].wait()
        for r in range(0, obs, 16):
            total = acc[r : r + 16, 0:levels]
            for c in range(i * per, (i + 1) * per):
                total = total + w[r : r + 16, c : c + 1] * kbuf[c, r : r + 16, :].astype(F32)
            acc[r : r + 16, 0:levels] = total

    for i in range(steps // 2):
        sums(i)
    for copy in small_copies[2:]:
        copy.wait()

    tr = jnp.broadcast_to(tile[...].astype(F32), (obs, obs))
    ri, ci = iota((obs, obs), 0), iota((obs, obs), 1)
    tc = jnp.sum(jnp.where(ri == ci, tr, 0.0), 1, keepdims=True)
    rank = jnp.sum(jnp.where((tc == tr) & (ri < ci), 1.0, 0.0), 0, keepdims=True)
    slot = (tile[...].astype(F32) * (2 * CAP) + rank).astype(jnp.int32)
    at = iota((rows_out, obs), 0)
    first_half, second_half = ones_where(at == slot), ones_where(at == slot + CAP)

    rows = iota((128, obs), 0)
    place = jnp.where(rows == base, frow[...].astype(F32), 0.0)
    place = jnp.where(rows == base + 1, fcol[...].astype(F32), place)
    place = jnp.where(rows == base + 2, crow[...].astype(F32), place)
    place = jnp.where(rows == base + 3, ccol[...].astype(F32), place)
    extra = dot(second_half, place.astype(BF16), NT)

    npred = predt.shape[0]
    ind = jnp.where(iota((kinds - npred, obs), 0) == scan[...], 1.0, 0.0)
    basist = jnp.concatenate([predt[...].astype(F32), ind], 0).astype(BF16)
    biast = dot(basist, wbf, NN)
    hi = biast.astype(BF16)
    lo = (biast - hi.astype(F32)).astype(BF16)
    for (e, f), place in zip(spreads, places):
        part = (dot(hi, e, NN) + dot(lo, f, NN)).astype(BF16)
        extra = extra + dot(place, part, NN)

    for i in range(steps // 2, steps):
        sums(i)
    rows = acc[...].astype(BF16)
    placed = dot(first_half, rows[:, 0:WIDE], NN) + dot(second_half, rows[:, WIDE:LANES], NN)
    out[:, 0 : WIDE - 128] = placed[:, 0 : WIDE - 128].astype(BF16)
    out[:, WIDE - 128 : WIDE] = (placed[:, WIDE - 128 : WIDE] + extra).astype(BF16)


def picks(slots, offset):
    q, r = iota((slots, 2 * slots), 0), iota((slots, 2 * slots), 1)
    return ones_where(r == (q // CAP) * (2 * CAP) + q % CAP + offset)


def chunk_kernel(got, chunk, *, levels, half):
    slots = got.shape[0] // 2
    q, r = iota((slots, 2 * slots), 0), iota((slots, 2 * slots), 1)
    pick = ones_where(r % (2 * CAP) == q % CAP + CAP)
    total = dot(pick, got[:, WIDE - 128 : WIDE], NN)
    first = levels - (LANES - 128) + 4
    lane = iota((slots, 128), 1)
    kept = 128 - first - half
    sums = jnp.where(lane < half, pltpu.roll(total, 128 - first, 1), 0.0)
    chunk[...] = sums + jnp.where(lane < kept, pltpu.roll(total, 128 - first - half, 1), 0.0)


def turn_kernel(got, out):
    slots = got.shape[0] // 2
    out[0:WIDE, :] = jnp.transpose(dot(picks(slots, 0), got[...], NN)).astype(BF16)
    rest = jnp.transpose(dot(picks(slots, CAP), got[...], NN))
    out[WIDE:VROWS, :] = rest[0 : VROWS - WIDE, :].astype(BF16)


def prep_kernel(first_row, a0, a1, a2, a3, spill, colw, roww, *, levels):
    refs = (a0, a1, a2, a3)
    tops = jnp.concatenate([ref[VROWS - 16 : VROWS, :].astype(F32) for ref in refs], 1)
    at = levels - (VROWS - 16)
    fr, fc = tops[at : at + 1, :], tops[at + 1 : at + 2, :]
    row, col = tops[at + 2 : at + 3, :].astype(jnp.int32), tops[at + 3 : at + 4, :].astype(jnp.int32)
    n = fr.shape[1]
    cols = iota((GC, n), 0)
    cw = jnp.where(cols == col, 1.0 - fc, jnp.where(cols == col + 1, fc, 0.0)).astype(BF16)
    colw[...] = cw
    rel = iota((BLOCK, n), 0) + first_row[0]
    roww[...] = jnp.where(rel == row, 1.0 - fr, 0.0) + jnp.where(rel == row + 1, fr, 0.0)
    last = jnp.where(row == GR - 1, fr, 0.0)
    part = a0.shape[1]
    out = jnp.zeros((VROWS, GC), F32)
    for j, ref in enumerate(refs):
        cols = slice(j * part, (j + 1) * part)
        lhs = (ref[...].astype(F32) * last[:, cols]).astype(BF16)
        out = out + dot(lhs, cw[:, cols], NT)
    spill[...] = out.astype(BF16)


def grid_kernel(a0, a1, a2, a3, colw, roww, out):
    part = a0.shape[1]
    for lo, hi in PARTS:
        total = jnp.zeros(((hi - lo) * BLOCK, GC), F32)
        for j, ref in enumerate((a0, a1, a2, a3)):
            cols = slice(j * part, (j + 1) * part)
            lhs = ref[lo:hi, :].astype(F32)[:, None, :] * roww[:, cols][None, :, :]
            lhs = lhs.reshape((hi - lo) * BLOCK, part).astype(BF16)
            total = total + dot(lhs, colw[:, cols], NT)
        out[lo:hi] = total.reshape(hi - lo, BLOCK, GC)


def join_kernel(grid, spill, out, joined, sems):
    levels = out.shape[0]
    copies = []
    for i, (lo, hi) in enumerate(PARTS):
        first = iota((hi - lo, BLOCK, GC), 1) == 0
        joined[lo:hi] = grid[lo:hi] + jnp.where(first, spill[lo:hi, :].astype(F32)[:, None, :], 0.0)
        size = min(hi, levels) - lo
        copies.append(pltpu.make_async_copy(joined.at[pl.ds(lo, size)], out.at[pl.ds(lo, size)], sems.at[i]))
        copies[i].start()
    for copy in copies:
        copy.wait()


def slot_bias_kernel(got, out, *, half):
    t = jnp.transpose(got[...])
    n = got.shape[0] // 2
    out[0:half, :] = t[0:half, 0:n]
    out[half : 2 * half, :] = t[0:half, n : 2 * n]


def bias_kernel(b0, b1, b2, b3, out, *, scale):
    out[...] = ((b0[...] + b1[...]) + (b2[...] + b3[...])) * scale


VM = pl.BlockSpec(memory_space=pltpu.VMEM)
HBM = pl.BlockSpec(memory_space=pltpu.HBM)


def per_device(
    departure, inv_var, k_matrix, frac_row, frac_col, dest_tile, cell_row, cell_col, predictors, scan_pos
):
    n_tile = lax.axis_size("tile")
    n_slot = lax.axis_size("slot")
    obs, chans, levels = k_matrix.shape
    slots = n_tile * CAP
    params = pltpu.CompilerParams(vmem_limit_bytes=VMEM)
    tight = pltpu.CompilerParams(vmem_limit_bytes=56 * 1024 * 1024)
    steps = 10
    flat = lambda x: x.reshape(1, obs)
    small = (
        departure,
        inv_var.reshape(1, chans),
        flat(dest_tile),
        flat(frac_row),
        flat(frac_col),
        flat(cell_row),
        flat(cell_col),
        predictors.T,
        flat(scan_pos),
    )
    send = pl.pallas_call(
        functools.partial(send_kernel, steps=steps),
        out_shape=jax.ShapeDtypeStruct((2 * slots, WIDE), BF16),
        in_specs=[HBM] * (1 + len(small)),
        out_specs=VM,
        scratch_shapes=[pltpu.VMEM(x.shape, x.dtype) for x in small]
        + [
            pltpu.VMEM((chans, obs, levels), BF16),
            pltpu.VMEM((obs, LANES), F32),
            pltpu.SemaphoreType.DMA((steps,)),
            pltpu.SemaphoreType.DMA((len(small),)),
        ],
        compiler_params=tight,
        name="send",
    )(jnp.transpose(k_matrix, (1, 0, 2)), *small)
    got = lax.all_to_all(send.reshape(n_tile, 2 * CAP, WIDE), "tile", 0, 0, tiled=True).reshape(2 * slots, WIDE)
    turned = pl.pallas_call(
        turn_kernel,
        out_shape=jax.ShapeDtypeStruct((VROWS, slots), BF16),
        in_specs=[VM],
        out_specs=VM,
        compiler_params=params,
        name="turn",
    )(got)

    def around(x):
        return [x] + [lax.ppermute(x, "slot", [(i, (i + d) % n_slot) for i in range(n_slot)]) for d in (1, 3, 2)]

    blocks = around(turned)
    chunk = pl.pallas_call(
        functools.partial(chunk_kernel, levels=levels, half=chans // 2),
        out_shape=jax.ShapeDtypeStruct((slots, 128), F32),
        in_specs=[VM],
        out_specs=VM,
        compiler_params=params,
        name="chunk",
    )(got)
    chunks = lax.all_to_all(chunk.reshape(n_tile, CAP, 128), "tile", 0, 0, tiled=True).reshape(slots, 128)
    total = n_slot * slots
    first_row = (lax.axis_index("slot") * BLOCK).astype(jnp.int32).reshape(1)
    spill, colw, roww = pl.pallas_call(
        functools.partial(prep_kernel, levels=levels),
        out_shape=(
            jax.ShapeDtypeStruct((VROWS, GC), BF16),
            jax.ShapeDtypeStruct((GC, total), BF16),
            jax.ShapeDtypeStruct((BLOCK, total), F32),
        ),
        in_specs=[pl.BlockSpec(memory_space=pltpu.SMEM)] + [VM] * 4,
        out_specs=(VM,) * 3,
        compiler_params=params,
        name="prep",
    )(first_row, *blocks)
    pairs = [(t * n_slot, ((t + 1) % n_tile) * n_slot) for t in range(n_tile)]
    arrived = lax.ppermute(spill, ("tile", "slot"), pairs)
    own = pl.pallas_call(
        grid_kernel,
        out_shape=jax.ShapeDtypeStruct((VROWS, BLOCK, GC), F32),
        in_specs=[VM] * 6,
        out_specs=VM,
        compiler_params=params,
        name="grid",
    )(*blocks, colw, roww)
    own, chunks = lax.optimization_barrier((own, chunks))
    slot_bias = pl.pallas_call(
        functools.partial(slot_bias_kernel, half=chans // 2),
        out_shape=jax.ShapeDtypeStruct((chans, 128), F32),
        in_specs=[VM],
        out_specs=VM,
        compiler_params=params,
        name="slot_bias",
    )(chunks)
    biases = around(slot_bias)
    grid = pl.pallas_call(
        join_kernel,
        out_shape=jax.ShapeDtypeStruct((levels, BLOCK, GC), F32),
        in_specs=[VM] * 2,
        out_specs=HBM,
        scratch_shapes=[pltpu.VMEM((VROWS, BLOCK, GC), F32), pltpu.SemaphoreType.DMA((len(PARTS),))],
        compiler_params=params,
        name="join",
    )(own, arrived)
    *biases, grid = lax.optimization_barrier((*biases, grid))
    bias = pl.pallas_call(
        functools.partial(bias_kernel, scale=1.0 / math.sqrt(obs * n_tile * n_slot)),
        out_shape=jax.ShapeDtypeStruct((chans, 128), F32),
        in_specs=[VM] * 4,
        out_specs=VM,
        compiler_params=params,
        name="bias",
    )(*biases)
    return jnp.transpose(grid, (1, 2, 0)), bias


def solution(mesh):
    both = ("tile", "slot")
    placed = (
        P(both, None),
        P(),
        P(both, None, None),
        P(both),
        P(both),
        P(both, None),
        P(both),
        P(both),
        P(both, None),
        P(both),
    )
    return jax.shard_map(
        per_device,
        mesh=mesh,
        in_specs=placed,
        out_specs=(P(both, None, None), P()),
        check_vma=False,
    )
```

```python
import functools
import math

import jax
import jax.numpy as jnp
from jax import lax
from jax.experimental import pallas as pl
from jax.experimental.pallas import tpu as pltpu
from jax.sharding import PartitionSpec as P

F32 = jnp.float32
BF16 = jnp.bfloat16
NT = (((1,), (1,)), ((), ()))
NN = (((1,), (0,)), ((), ()))

CAP = 4
GR = 32
GC = 256
LANES = 512
WIDE = LANES // 2
VROWS = 416
PARTS = ((0, 128), (128, 256), (256, 336), (336, 416))
EARLY = 2
BLOCK = 8
VMEM = 24 * 1024 * 1024


def iota(shape, dim):
    return lax.broadcasted_iota(jnp.int32, shape, dim)


def dot(a, b, dims):
    return lax.dot_general(a, b, dims, preferred_element_type=F32)


def ones_where(mask):
    return jnp.where(mask, 1.0, 0.0).astype(BF16)


def send_kernel(*refs, steps):
    k_hbm, small_hbm, out, small, kbuf, acc, sems, small_sems = refs[0], refs[1:10], *refs[10:11], refs[11:20], *refs[20:]
    chans, obs, levels = k_hbm.shape
    per = chans // steps
    small_copies = [
        pltpu.make_async_copy(src, dst, small_sems.at[i]) for i, (src, dst) in enumerate(zip(small_hbm, small))
    ]
    copies = [
        pltpu.make_async_copy(k_hbm.at[pl.ds(i * per, per)], kbuf.at[pl.ds(i * per, per)], sems.at[i])
        for i in range(steps)
    ]
    for copy in small_copies[:2] + copies[:2] + small_copies[2:] + copies[2:]:
        copy.start()
    dep, inv, tile, frow, fcol, crow, ccol, predt, scan = small
    rows_out = out.shape[0]

    kinds = 128
    half = chans // 2
    base = levels - (LANES - 128)
    first = base + 4
    er, ec = iota((chans, 128), 0), iota((chans, 128), 1)
    qr, qk = iota((rows_out, kinds), 0), iota((rows_out, kinds), 1)
    spreads, places = [], []
    for h in range(2):
        mine = (er >= h * half) & (er < (h + 1) * half)
        e = ones_where((ec == er - h * half + first) & mine)
        f = ones_where((ec == er - h * half + first + half) & mine)
        spreads.append((e, f))
        q = qk + h * kinds
        places.append(ones_where(qr == (q // CAP) * (2 * CAP) + CAP + q % CAP))
    acc[...] = jnp.zeros(acc.shape, F32)
    for copy in small_copies[:2]:
        copy.wait()
    wbf = (dep[...].astype(F32) * inv[...]).astype(BF16)
    w = wbf.astype(F32)

    def sums(i):
        copies[i].wait()
        for r in range(0, obs, 16):
            total = acc[r : r + 16, 0:levels]
            for c in range(i * per, (i + 1) * per):
                total = total + w[r : r + 16, c : c + 1] * kbuf[c, r : r + 16, :].astype(F32)
            acc[r : r + 16, 0:levels] = total

    for i in range(steps // 2):
        sums(i)
    for copy in small_copies[2:]:
        copy.wait()

    tr = jnp.broadcast_to(tile[...].astype(F32), (obs, obs))
    ri, ci = iota((obs, obs), 0), iota((obs, obs), 1)
    tc = jnp.sum(jnp.where(ri == ci, tr, 0.0), 1, keepdims=True)
    rank = jnp.sum(jnp.where((tc == tr) & (ri < ci), 1.0, 0.0), 0, keepdims=True)
    slot = (tile[...].astype(F32) * (2 * CAP) + rank).astype(jnp.int32)
    at = iota((rows_out, obs), 0)
    first_half, second_half = ones_where(at == slot), ones_where(at == slot + CAP)

    rows = iota((128, obs), 0)
    place = jnp.where(rows == base, frow[...].astype(F32), 0.0)
    place = jnp.where(rows == base + 1, fcol[...].astype(F32), place)
    place = jnp.where(rows == base + 2, crow[...].astype(F32), place)
    place = jnp.where(rows == base + 3, ccol[...].astype(F32), place)
    extra = dot(second_half, place.astype(BF16), NT)

    npred = predt.shape[0]
    ind = jnp.where(iota((kinds - npred, obs), 0) == scan[...], 1.0, 0.0)
    basist = jnp.concatenate([predt[...].astype(F32), ind], 0).astype(BF16)
    biast = dot(basist, wbf, NN)
    hi = biast.astype(BF16)
    lo = (biast - hi.astype(F32)).astype(BF16)
    for (e, f), place in zip(spreads, places):
        part = (dot(hi, e, NN) + dot(lo, f, NN)).astype(BF16)
        extra = extra + dot(place, part, NN)

    for i in range(steps // 2, steps):
        sums(i)
    rows = acc[...].astype(BF16)
    placed = dot(first_half, rows[:, 0:WIDE], NN) + dot(second_half, rows[:, WIDE:LANES], NN)
    out[:, 0 : WIDE - 128] = placed[:, 0 : WIDE - 128].astype(BF16)
    out[:, WIDE - 128 : WIDE] = (placed[:, WIDE - 128 : WIDE] + extra).astype(BF16)


def picks(slots, offset):
    q, r = iota((slots, 2 * slots), 0), iota((slots, 2 * slots), 1)
    return ones_where(r == (q // CAP) * (2 * CAP) + q % CAP + offset)


def chunk_kernel(got, chunk, *, levels, half):
    slots = got.shape[0] // 2
    q, r = iota((slots, 2 * slots), 0), iota((slots, 2 * slots), 1)
    pick = ones_where(r % (2 * CAP) == q % CAP + CAP)
    total = dot(pick, got[:, WIDE - 128 : WIDE], NN)
    first = levels - (LANES - 128) + 4
    lane = iota((slots, 128), 1)
    kept = 128 - first - half
    sums = jnp.where(lane < half, pltpu.roll(total, 128 - first, 1), 0.0)
    chunk[...] = sums + jnp.where(lane < kept, pltpu.roll(total, 128 - first - half, 1), 0.0)


def turn_kernel(got, out):
    slots = got.shape[0] // 2
    out[0:WIDE, :] = jnp.transpose(dot(picks(slots, 0), got[...], NN)).astype(BF16)
    rest = jnp.transpose(dot(picks(slots, CAP), got[...], NN))
    out[WIDE:VROWS, :] = rest[0 : VROWS - WIDE, :].astype(BF16)


def prep_kernel(first_row, a0, a1, a2, a3, spill, colw, roww, early, late, *, levels):
    refs = (a0, a1, a2, a3)
    tops = jnp.concatenate([ref[VROWS - 16 : VROWS, :].astype(F32) for ref in refs], 1)
    at = levels - (VROWS - 16)
    fr, fc = tops[at : at + 1, :], tops[at + 1 : at + 2, :]
    row, col = tops[at + 2 : at + 3, :].astype(jnp.int32), tops[at + 3 : at + 4, :].astype(jnp.int32)
    n = fr.shape[1]
    cols = iota((GC, n), 0)
    cw = jnp.where(cols == col, 1.0 - fc, jnp.where(cols == col + 1, fc, 0.0)).astype(BF16)
    colw[...] = cw
    rel = iota((BLOCK, n), 0) + first_row[0]
    roww[...] = jnp.where(rel == row, 1.0 - fr, 0.0) + jnp.where(rel == row + 1, fr, 0.0)
    last = jnp.where(row == GR - 1, fr, 0.0)
    part = a0.shape[1]
    out = jnp.zeros((VROWS, GC), F32)
    for j, ref in enumerate(refs):
        cols = slice(j * part, (j + 1) * part)
        early[:, cols] = ref[0 : early.shape[0], :]
        late[:, cols] = ref[early.shape[0] : VROWS, :]
        lhs = (ref[...].astype(F32) * last[:, cols]).astype(BF16)
        out = out + dot(lhs, cw[:, cols], NT)
    spill[...] = out.astype(BF16)


def grid_part(rows, colw, roww, lo, hi):
    lhs = rows[lo:hi, :].astype(F32)[:, None, :] * roww[...][None, :, :]
    lhs = lhs.reshape((hi - lo) * BLOCK, rows.shape[1]).astype(BF16)
    return dot(lhs, colw[...], NT).reshape(hi - lo, BLOCK, GC)


def grid_kernel(rows, colw, roww, out):
    for lo, hi in PARTS[:EARLY]:
        out[lo:hi] = grid_part(rows, colw, roww, lo, hi)


def join_kernel(grid, rows, colw, roww, spill, out, joined, sems):
    levels = out.shape[0]
    copies = []
    for i, (lo, hi) in enumerate(PARTS):
        first = iota((hi - lo, BLOCK, GC), 1) == 0
        own = grid[lo:hi] if i < EARLY else grid_part(rows, colw, roww, lo - PARTS[EARLY][0], hi - PARTS[EARLY][0])
        joined[lo:hi] = own + jnp.where(first, spill[lo:hi, :].astype(F32)[:, None, :], 0.0)
        size = min(hi, levels) - lo
        copies.append(pltpu.make_async_copy(joined.at[pl.ds(lo, size)], out.at[pl.ds(lo, size)], sems.at[i]))
        copies[i].start()
    for copy in copies:
        copy.wait()


def slot_bias_kernel(got, out, *, half):
    t = jnp.transpose(got[...])
    n = got.shape[0] // 2
    out[0:half, :] = t[0:half, 0:n]
    out[half : 2 * half, :] = t[0:half, n : 2 * n]


def bias_kernel(b0, b1, b2, b3, out, *, scale):
    out[...] = ((b0[...] + b1[...]) + (b2[...] + b3[...])) * scale


VM = pl.BlockSpec(memory_space=pltpu.VMEM)
HBM = pl.BlockSpec(memory_space=pltpu.HBM)


def per_device(
    departure, inv_var, k_matrix, frac_row, frac_col, dest_tile, cell_row, cell_col, predictors, scan_pos
):
    n_tile = lax.axis_size("tile")
    n_slot = lax.axis_size("slot")
    obs, chans, levels = k_matrix.shape
    slots = n_tile * CAP
    params = pltpu.CompilerParams(vmem_limit_bytes=VMEM)
    tight = pltpu.CompilerParams(vmem_limit_bytes=56 * 1024 * 1024)
    steps = 10
    flat = lambda x: x.reshape(1, obs)
    small = (
        departure,
        inv_var.reshape(1, chans),
        flat(dest_tile),
        flat(frac_row),
        flat(frac_col),
        flat(cell_row),
        flat(cell_col),
        predictors.T,
        flat(scan_pos),
    )
    send = pl.pallas_call(
        functools.partial(send_kernel, steps=steps),
        out_shape=jax.ShapeDtypeStruct((2 * slots, WIDE), BF16),
        in_specs=[HBM] * (1 + len(small)),
        out_specs=VM,
        scratch_shapes=[pltpu.VMEM(x.shape, x.dtype) for x in small]
        + [
            pltpu.VMEM((chans, obs, levels), BF16),
            pltpu.VMEM((obs, LANES), F32),
            pltpu.SemaphoreType.DMA((steps,)),
            pltpu.SemaphoreType.DMA((len(small),)),
        ],
        compiler_params=tight,
        name="send",
    )(jnp.transpose(k_matrix, (1, 0, 2)), *small)
    got = lax.all_to_all(send.reshape(n_tile, 2 * CAP, WIDE), "tile", 0, 0, tiled=True).reshape(2 * slots, WIDE)
    turned = pl.pallas_call(
        turn_kernel,
        out_shape=jax.ShapeDtypeStruct((VROWS, slots), BF16),
        in_specs=[VM],
        out_specs=VM,
        compiler_params=params,
        name="turn",
    )(got)

    def around(x):
        return [x] + [lax.ppermute(x, "slot", [(i, (i + d) % n_slot) for i in range(n_slot)]) for d in (1, 3, 2)]

    blocks = around(turned)
    chunk = pl.pallas_call(
        functools.partial(chunk_kernel, levels=levels, half=chans // 2),
        out_shape=jax.ShapeDtypeStruct((slots, 128), F32),
        in_specs=[VM],
        out_specs=VM,
        compiler_params=params,
        name="chunk",
    )(got)
    chunks = lax.all_to_all(chunk.reshape(n_tile, CAP, 128), "tile", 0, 0, tiled=True).reshape(slots, 128)
    total = n_slot * slots
    split = PARTS[EARLY][0]
    first_row = (lax.axis_index("slot") * BLOCK).astype(jnp.int32).reshape(1)
    spill, colw, roww, early, late = pl.pallas_call(
        functools.partial(prep_kernel, levels=levels),
        out_shape=(
            jax.ShapeDtypeStruct((VROWS, GC), BF16),
            jax.ShapeDtypeStruct((GC, total), BF16),
            jax.ShapeDtypeStruct((BLOCK, total), F32),
            jax.ShapeDtypeStruct((split, total), BF16),
            jax.ShapeDtypeStruct((VROWS - split, total), BF16),
        ),
        in_specs=[pl.BlockSpec(memory_space=pltpu.SMEM)] + [VM] * 4,
        out_specs=(VM,) * 5,
        compiler_params=params,
        name="prep",
    )(first_row, *blocks)
    pairs = [(t * n_slot, ((t + 1) % n_tile) * n_slot) for t in range(n_tile)]
    arrived = lax.ppermute(spill, ("tile", "slot"), pairs)
    own = pl.pallas_call(
        grid_kernel,
        out_shape=jax.ShapeDtypeStruct((split, BLOCK, GC), F32),
        in_specs=[VM] * 3,
        out_specs=VM,
        compiler_params=params,
        name="grid",
    )(early, colw, roww)
    own, chunks = lax.optimization_barrier((own, chunks))
    slot_bias = pl.pallas_call(
        functools.partial(slot_bias_kernel, half=chans // 2),
        out_shape=jax.ShapeDtypeStruct((chans, 128), F32),
        in_specs=[VM],
        out_specs=VM,
        compiler_params=params,
        name="slot_bias",
    )(chunks)
    biases = around(slot_bias)
    grid = pl.pallas_call(
        join_kernel,
        out_shape=jax.ShapeDtypeStruct((levels, BLOCK, GC), F32),
        in_specs=[VM] * 5,
        out_specs=HBM,
        scratch_shapes=[pltpu.VMEM((VROWS, BLOCK, GC), F32), pltpu.SemaphoreType.DMA((len(PARTS),))],
        compiler_params=params,
        name="join",
    )(own, late, colw, roww, arrived)
    *biases, grid = lax.optimization_barrier((*biases, grid))
    bias = pl.pallas_call(
        functools.partial(bias_kernel, scale=1.0 / math.sqrt(obs * n_tile * n_slot)),
        out_shape=jax.ShapeDtypeStruct((chans, 128), F32),
        in_specs=[VM] * 4,
        out_specs=VM,
        compiler_params=params,
        name="bias",
    )(*biases)
    return jnp.transpose(grid, (1, 2, 0)), bias


def solution(mesh):
    both = ("tile", "slot")
    placed = (
        P(both, None),
        P(),
        P(both, None, None),
        P(both),
        P(both),
        P(both, None),
        P(both),
        P(both),
        P(both, None),
        P(both),
    )
    return jax.shard_map(
        per_device,
        mesh=mesh,
        in_specs=placed,
        out_specs=(P(both, None, None), P()),
        check_vma=False,
    )
```

```python
import functools
import math

import jax
import jax.numpy as jnp
from jax import lax
from jax.experimental import pallas as pl
from jax.experimental.pallas import tpu as pltpu
from jax.sharding import PartitionSpec as P

F32 = jnp.float32
BF16 = jnp.bfloat16
NT = (((1,), (1,)), ((), ()))
NN = (((1,), (0,)), ((), ()))

CAP = 4
GR = 32
GC = 256
LANES = 512
WIDE = LANES // 2
VROWS = 416
PARTS = ((0, 128), (128, 256), (256, 368), (368, 416))
EARLY = 2
OUT_BLOCKS = 4
BLOCK = 8
VMEM = 24 * 1024 * 1024


def iota(shape, dim):
    return lax.broadcasted_iota(jnp.int32, shape, dim)


def dot(a, b, dims):
    return lax.dot_general(a, b, dims, preferred_element_type=F32)


def ones_where(mask):
    return jnp.where(mask, 1.0, 0.0).astype(BF16)


def send_kernel(*refs, steps):
    k_hbm, small_hbm, out, small = refs[0], refs[1:10], refs[10], refs[11:20]
    kbuf, acc, placed, sems, small_sems, out_sems = refs[20:]
    chans, obs, levels = k_hbm.shape
    per = chans // steps
    small_copies = [
        pltpu.make_async_copy(src, dst, small_sems.at[i]) for i, (src, dst) in enumerate(zip(small_hbm, small))
    ]
    copies = [
        pltpu.make_async_copy(k_hbm.at[pl.ds(i * per, per)], kbuf.at[pl.ds(i * per, per)], sems.at[i])
        for i in range(steps)
    ]
    for copy in small_copies[:2] + copies[:2] + small_copies[2:] + copies[2:]:
        copy.start()
    dep, inv, tile, frow, fcol, crow, ccol, predt, scan = small
    rows_out = out.shape[0]

    kinds = 128
    half = chans // 2
    base = levels - (LANES - 128)
    first = base + 4
    er, ec = iota((chans, 128), 0), iota((chans, 128), 1)
    qr, qk = iota((rows_out, kinds), 0), iota((rows_out, kinds), 1)
    spreads, places = [], []
    for h in range(2):
        mine = (er >= h * half) & (er < (h + 1) * half)
        e = ones_where((ec == er - h * half + first) & mine)
        f = ones_where((ec == er - h * half + first + half) & mine)
        spreads.append((e, f))
        q = qk + h * kinds
        places.append(ones_where(qr == (q // CAP) * (2 * CAP) + CAP + q % CAP))
    acc[...] = jnp.zeros(acc.shape, F32)
    for copy in small_copies[:2]:
        copy.wait()
    wbf = (dep[...].astype(F32) * inv[...]).astype(BF16)
    w = wbf.astype(F32)

    def sums(i):
        copies[i].wait()
        for r in range(0, obs, 16):
            total = acc[r : r + 16, 0:levels]
            for c in range(i * per, (i + 1) * per):
                total = total + w[r : r + 16, c : c + 1] * kbuf[c, r : r + 16, :].astype(F32)
            acc[r : r + 16, 0:levels] = total

    for i in range(steps // 2):
        sums(i)
    for copy in small_copies[2:]:
        copy.wait()

    tr = jnp.broadcast_to(tile[...].astype(F32), (obs, obs))
    ri, ci = iota((obs, obs), 0), iota((obs, obs), 1)
    tc = jnp.sum(jnp.where(ri == ci, tr, 0.0), 1, keepdims=True)
    rank = jnp.sum(jnp.where((tc == tr) & (ri < ci), 1.0, 0.0), 0, keepdims=True)
    slot = (tile[...].astype(F32) * (2 * CAP) + rank).astype(jnp.int32)
    at = iota((rows_out, obs), 0)
    first_half, second_half = ones_where(at == slot), ones_where(at == slot + CAP)

    rows = iota((128, obs), 0)
    place = jnp.where(rows == base, frow[...].astype(F32), 0.0)
    place = jnp.where(rows == base + 1, fcol[...].astype(F32), place)
    place = jnp.where(rows == base + 2, crow[...].astype(F32), place)
    place = jnp.where(rows == base + 3, ccol[...].astype(F32), place)
    extra = dot(second_half, place.astype(BF16), NT)

    npred = predt.shape[0]
    ind = jnp.where(iota((kinds - npred, obs), 0) == scan[...], 1.0, 0.0)
    basist = jnp.concatenate([predt[...].astype(F32), ind], 0).astype(BF16)
    biast = dot(basist, wbf, NN)
    hi = biast.astype(BF16)
    lo = (biast - hi.astype(F32)).astype(BF16)
    for (e, f), place in zip(spreads, places):
        part = (dot(hi, e, NN) + dot(lo, f, NN)).astype(BF16)
        extra = extra + dot(place, part, NN)

    for i in range(steps // 2, steps):
        sums(i)
    rows = acc[...].astype(BF16)
    size = rows_out // OUT_BLOCKS
    out_copies = []
    for i in range(OUT_BLOCKS):
        at = slice(i * size, (i + 1) * size)
        block = dot(first_half[at, :], rows[:, 0:WIDE], NN) + dot(second_half[at, :], rows[:, WIDE:LANES], NN)
        placed[at, 0 : WIDE - 128] = block[:, 0 : WIDE - 128].astype(BF16)
        placed[at, WIDE - 128 : WIDE] = (block[:, WIDE - 128 : WIDE] + extra[at, :]).astype(BF16)
        here = pl.ds(i * size, size)
        out_copies.append(pltpu.make_async_copy(placed.at[here], out.at[here], out_sems.at[i]))
        out_copies[i].start()
    for copy in out_copies:
        copy.wait()


def picks(slots, offset):
    q, r = iota((slots, 2 * slots), 0), iota((slots, 2 * slots), 1)
    return ones_where(r == (q // CAP) * (2 * CAP) + q % CAP + offset)


def chunk_kernel(got, chunk, *, levels, half):
    slots = got.shape[0] // 2
    q, r = iota((slots, 2 * slots), 0), iota((slots, 2 * slots), 1)
    pick = ones_where(r % (2 * CAP) == q % CAP + CAP)
    total = dot(pick, got[:, WIDE - 128 : WIDE], NN)
    first = levels - (LANES - 128) + 4
    lane = iota((slots, 128), 1)
    kept = 128 - first - half
    sums = jnp.where(lane < half, pltpu.roll(total, 128 - first, 1), 0.0)
    chunk[...] = sums + jnp.where(lane < kept, pltpu.roll(total, 128 - first - half, 1), 0.0)


def turn_kernel(got, out):
    slots = got.shape[0] // 2
    out[0:WIDE, :] = jnp.transpose(dot(picks(slots, 0), got[...], NN)).astype(BF16)
    rest = jnp.transpose(dot(picks(slots, CAP), got[...], NN))
    out[WIDE:VROWS, :] = rest[0 : VROWS - WIDE, :].astype(BF16)


def prep_kernel(first_row, a0, a1, a2, a3, spill, colw, roww, early, late, *, levels):
    refs = (a0, a1, a2, a3)
    tops = jnp.concatenate([ref[VROWS - 16 : VROWS, :].astype(F32) for ref in refs], 1)
    at = levels - (VROWS - 16)
    fr, fc = tops[at : at + 1, :], tops[at + 1 : at + 2, :]
    row, col = tops[at + 2 : at + 3, :].astype(jnp.int32), tops[at + 3 : at + 4, :].astype(jnp.int32)
    n = fr.shape[1]
    cols = iota((GC, n), 0)
    cw = jnp.where(cols == col, 1.0 - fc, jnp.where(cols == col + 1, fc, 0.0)).astype(BF16)
    colw[...] = cw
    rel = iota((BLOCK, n), 0) + first_row[0]
    roww[...] = jnp.where(rel == row, 1.0 - fr, 0.0) + jnp.where(rel == row + 1, fr, 0.0)
    last = jnp.where(row == GR - 1, fr, 0.0)
    part = a0.shape[1]
    out = jnp.zeros((VROWS, GC), F32)
    for j, ref in enumerate(refs):
        cols = slice(j * part, (j + 1) * part)
        early[:, cols] = ref[0 : early.shape[0], :]
        late[:, cols] = ref[early.shape[0] : VROWS, :]
        lhs = (ref[...].astype(F32) * last[:, cols]).astype(BF16)
        out = out + dot(lhs, cw[:, cols], NT)
    spill[...] = out.astype(BF16)


def grid_part(rows, colw, roww, lo, hi):
    lhs = rows[lo:hi, :].astype(F32)[:, None, :] * roww[...][None, :, :]
    lhs = lhs.reshape((hi - lo) * BLOCK, rows.shape[1]).astype(BF16)
    return dot(lhs, colw[...], NT).reshape(hi - lo, BLOCK, GC)


def grid_kernel(rows, colw, roww, out):
    for lo, hi in PARTS[:EARLY]:
        out[lo:hi] = grid_part(rows, colw, roww, lo, hi)


def join_kernel(grid, rows, colw, roww, spill, out, joined, sems):
    levels = out.shape[0]
    copies = []
    for i, (lo, hi) in enumerate(PARTS):
        first = iota((hi - lo, BLOCK, GC), 1) == 0
        own = grid[lo:hi] if i < EARLY else grid_part(rows, colw, roww, lo - PARTS[EARLY][0], hi - PARTS[EARLY][0])
        joined[lo:hi] = own + jnp.where(first, spill[lo:hi, :].astype(F32)[:, None, :], 0.0)
        size = min(hi, levels) - lo
        copies.append(pltpu.make_async_copy(joined.at[pl.ds(lo, size)], out.at[pl.ds(lo, size)], sems.at[i]))
        copies[i].start()
    for copy in copies:
        copy.wait()


def slot_bias_kernel(got, out, *, half):
    t = jnp.transpose(got[...])
    n = got.shape[0] // 2
    out[0:half, :] = t[0:half, 0:n]
    out[half : 2 * half, :] = t[0:half, n : 2 * n]


def bias_kernel(b0, b1, b2, b3, out, *, scale):
    out[...] = ((b0[...] + b1[...]) + (b2[...] + b3[...])) * scale


VM = pl.BlockSpec(memory_space=pltpu.VMEM)
HBM = pl.BlockSpec(memory_space=pltpu.HBM)


def per_device(
    departure, inv_var, k_matrix, frac_row, frac_col, dest_tile, cell_row, cell_col, predictors, scan_pos
):
    n_tile = lax.axis_size("tile")
    n_slot = lax.axis_size("slot")
    obs, chans, levels = k_matrix.shape
    slots = n_tile * CAP
    params = pltpu.CompilerParams(vmem_limit_bytes=VMEM)
    tight = pltpu.CompilerParams(vmem_limit_bytes=56 * 1024 * 1024)
    steps = 10
    flat = lambda x: x.reshape(1, obs)
    small = (
        departure,
        inv_var.reshape(1, chans),
        flat(dest_tile),
        flat(frac_row),
        flat(frac_col),
        flat(cell_row),
        flat(cell_col),
        predictors.T,
        flat(scan_pos),
    )
    send = pl.pallas_call(
        functools.partial(send_kernel, steps=steps),
        out_shape=jax.ShapeDtypeStruct((2 * slots, WIDE), BF16),
        in_specs=[HBM] * (1 + len(small)),
        out_specs=HBM,
        scratch_shapes=[pltpu.VMEM(x.shape, x.dtype) for x in small]
        + [
            pltpu.VMEM((chans, obs, levels), BF16),
            pltpu.VMEM((obs, LANES), F32),
            pltpu.VMEM((2 * slots, WIDE), BF16),
            pltpu.SemaphoreType.DMA((steps,)),
            pltpu.SemaphoreType.DMA((len(small),)),
            pltpu.SemaphoreType.DMA((OUT_BLOCKS,)),
        ],
        compiler_params=tight,
        name="send",
    )(jnp.transpose(k_matrix, (1, 0, 2)), *small)
    got = lax.all_to_all(send.reshape(n_tile, 2 * CAP, WIDE), "tile", 0, 0, tiled=True).reshape(2 * slots, WIDE)
    turned = pl.pallas_call(
        turn_kernel,
        out_shape=jax.ShapeDtypeStruct((VROWS, slots), BF16),
        in_specs=[VM],
        out_specs=VM,
        compiler_params=params,
        name="turn",
    )(got)

    def around(x, distances):
        return [x] + [lax.ppermute(x, "slot", [(i, (i + d) % n_slot) for i in range(n_slot)]) for d in distances]

    blocks = around(turned, (1, 3, 2))
    chunk = pl.pallas_call(
        functools.partial(chunk_kernel, levels=levels, half=chans // 2),
        out_shape=jax.ShapeDtypeStruct((slots, 128), F32),
        in_specs=[VM],
        out_specs=VM,
        compiler_params=params,
        name="chunk",
    )(got)
    chunks = lax.all_to_all(chunk.reshape(n_tile, CAP, 128), "tile", 0, 0, tiled=True).reshape(slots, 128)
    total = n_slot * slots
    split = PARTS[EARLY][0]
    first_row = (lax.axis_index("slot") * BLOCK).astype(jnp.int32).reshape(1)
    spill, colw, roww, early, late = pl.pallas_call(
        functools.partial(prep_kernel, levels=levels),
        out_shape=(
            jax.ShapeDtypeStruct((VROWS, GC), BF16),
            jax.ShapeDtypeStruct((GC, total), BF16),
            jax.ShapeDtypeStruct((BLOCK, total), F32),
            jax.ShapeDtypeStruct((split, total), BF16),
            jax.ShapeDtypeStruct((VROWS - split, total), BF16),
        ),
        in_specs=[pl.BlockSpec(memory_space=pltpu.SMEM)] + [VM] * 4,
        out_specs=(VM,) * 5,
        compiler_params=params,
        name="prep",
    )(first_row, *blocks)
    pairs = [(t * n_slot, ((t + 1) % n_tile) * n_slot) for t in range(n_tile)]
    arrived = lax.ppermute(spill, ("tile", "slot"), pairs)
    own = pl.pallas_call(
        grid_kernel,
        out_shape=jax.ShapeDtypeStruct((split, BLOCK, GC), F32),
        in_specs=[VM] * 3,
        out_specs=VM,
        compiler_params=params,
        name="grid",
    )(early, colw, roww)
    own, chunks = lax.optimization_barrier((own, chunks))
    slot_bias = pl.pallas_call(
        functools.partial(slot_bias_kernel, half=chans // 2),
        out_shape=jax.ShapeDtypeStruct((chans, 128), F32),
        in_specs=[VM],
        out_specs=VM,
        compiler_params=params,
        name="slot_bias",
    )(chunks)
    biases = around(slot_bias, (2, 1, 3))
    grid = pl.pallas_call(
        join_kernel,
        out_shape=jax.ShapeDtypeStruct((levels, BLOCK, GC), F32),
        in_specs=[VM] * 5,
        out_specs=HBM,
        scratch_shapes=[pltpu.VMEM((VROWS, BLOCK, GC), F32), pltpu.SemaphoreType.DMA((len(PARTS),))],
        compiler_params=params,
        name="join",
    )(own, late, colw, roww, arrived)
    *biases, grid = lax.optimization_barrier((*biases, grid))
    bias = pl.pallas_call(
        functools.partial(bias_kernel, scale=1.0 / math.sqrt(obs * n_tile * n_slot)),
        out_shape=jax.ShapeDtypeStruct((chans, 128), F32),
        in_specs=[VM] * 4,
        out_specs=VM,
        compiler_params=params,
        name="bias",
    )(*biases)
    return jnp.transpose(grid, (1, 2, 0)), bias


def solution(mesh):
    both = ("tile", "slot")
    placed = (
        P(both, None),
        P(),
        P(both, None, None),
        P(both),
        P(both),
        P(both, None),
        P(both),
        P(both),
        P(both, None),
        P(both),
    )
    return jax.shard_map(
        per_device,
        mesh=mesh,
        in_specs=placed,
        out_specs=(P(both, None, None), P()),
        check_vma=False,
    )
```

```python
import functools
import math

import jax
import jax.numpy as jnp
from jax import lax
from jax.experimental import pallas as pl
from jax.experimental.pallas import tpu as pltpu
from jax.sharding import PartitionSpec as P

F32 = jnp.float32
BF16 = jnp.bfloat16
NT = (((1,), (1,)), ((), ()))
NN = (((1,), (0,)), ((), ()))

CAP = 4
GR = 32
GC = 256
LANES = 512
WIDE = LANES // 2
VROWS = 416
PARTS = ((0, 128), (128, 256), (256, 336), (336, 416))
EARLY = 2
OUT_BLOCKS = 4
BLOCK = 8
VMEM = 24 * 1024 * 1024


def iota(shape, dim):
    return lax.broadcasted_iota(jnp.int32, shape, dim)


def dot(a, b, dims):
    return lax.dot_general(a, b, dims, preferred_element_type=F32)


def ones_where(mask):
    return jnp.where(mask, 1.0, 0.0).astype(BF16)


def send_kernel(*refs, steps):
    k_hbm, small_hbm, out, small = refs[0], refs[1:10], refs[10], refs[11:20]
    kbuf, acc, placed, sems, small_sems, out_sems = refs[20:]
    chans, obs, levels = k_hbm.shape
    per = chans // steps
    small_copies = [
        pltpu.make_async_copy(src, dst, small_sems.at[i]) for i, (src, dst) in enumerate(zip(small_hbm, small))
    ]
    copies = [
        pltpu.make_async_copy(k_hbm.at[pl.ds(i * per, per)], kbuf.at[pl.ds(i * per, per)], sems.at[i])
        for i in range(steps)
    ]
    for copy in small_copies[:2] + copies[:2] + small_copies[2:] + copies[2:]:
        copy.start()
    dep, inv, tile, frow, fcol, crow, ccol, predt, scan = small
    rows_out = out.shape[0]

    kinds = 128
    half = chans // 2
    base = levels - (LANES - 128)
    first = base + 4
    er, ec = iota((chans, 128), 0), iota((chans, 128), 1)
    qr, qk = iota((rows_out, kinds), 0), iota((rows_out, kinds), 1)
    spreads, places = [], []
    for h in range(2):
        mine = (er >= h * half) & (er < (h + 1) * half)
        e = ones_where((ec == er - h * half + first) & mine)
        f = ones_where((ec == er - h * half + first + half) & mine)
        spreads.append((e, f))
        q = qk + h * kinds
        places.append(ones_where(qr == (q // CAP) * (2 * CAP) + CAP + q % CAP))
    acc[...] = jnp.zeros(acc.shape, F32)
    for copy in small_copies[:2]:
        copy.wait()
    wbf = (dep[...].astype(F32) * inv[...]).astype(BF16)
    w = wbf.astype(F32)

    def sums(i):
        copies[i].wait()
        for r in range(0, obs, 16):
            total = acc[r : r + 16, 0:levels]
            for c in range(i * per, (i + 1) * per):
                total = total + w[r : r + 16, c : c + 1] * kbuf[c, r : r + 16, :].astype(F32)
            acc[r : r + 16, 0:levels] = total

    for i in range(steps // 2):
        sums(i)
    for copy in small_copies[2:]:
        copy.wait()

    tr = jnp.broadcast_to(tile[...].astype(F32), (obs, obs))
    ri, ci = iota((obs, obs), 0), iota((obs, obs), 1)
    tc = jnp.sum(jnp.where(ri == ci, tr, 0.0), 1, keepdims=True)
    rank = jnp.sum(jnp.where((tc == tr) & (ri < ci), 1.0, 0.0), 0, keepdims=True)
    slot = (tile[...].astype(F32) * (2 * CAP) + rank).astype(jnp.int32)
    at = iota((rows_out, obs), 0)
    first_half, second_half = ones_where(at == slot), ones_where(at == slot + CAP)

    rows = iota((128, obs), 0)
    place = jnp.where(rows == base, frow[...].astype(F32), 0.0)
    place = jnp.where(rows == base + 1, fcol[...].astype(F32), place)
    place = jnp.where(rows == base + 2, crow[...].astype(F32), place)
    place = jnp.where(rows == base + 3, ccol[...].astype(F32), place)
    extra = dot(second_half, place.astype(BF16), NT)

    npred = predt.shape[0]
    ind = jnp.where(iota((kinds - npred, obs), 0) == scan[...], 1.0, 0.0)
    basist = jnp.concatenate([predt[...].astype(F32), ind], 0).astype(BF16)
    biast = dot(basist, wbf, NN)
    hi = biast.astype(BF16)
    lo = (biast - hi.astype(F32)).astype(BF16)
    for (e, f), place in zip(spreads, places):
        part = (dot(hi, e, NN) + dot(lo, f, NN)).astype(BF16)
        extra = extra + dot(place, part, NN)

    for i in range(steps // 2, steps):
        sums(i)
    rows = acc[...].astype(BF16)
    size = rows_out // OUT_BLOCKS
    out_copies = []
    for i in range(OUT_BLOCKS):
        at = slice(i * size, (i + 1) * size)
        block = dot(first_half[at, :], rows[:, 0:WIDE], NN) + dot(second_half[at, :], rows[:, WIDE:LANES], NN)
        placed[at, 0 : WIDE - 128] = block[:, 0 : WIDE - 128].astype(BF16)
        placed[at, WIDE - 128 : WIDE] = (block[:, WIDE - 128 : WIDE] + extra[at, :]).astype(BF16)
        here = pl.ds(i * size, size)
        out_copies.append(pltpu.make_async_copy(placed.at[here], out.at[here], out_sems.at[i]))
        out_copies[i].start()
    for copy in out_copies:
        copy.wait()


def picks(slots, offset):
    q, r = iota((slots, 2 * slots), 0), iota((slots, 2 * slots), 1)
    return ones_where(r == (q // CAP) * (2 * CAP) + q % CAP + offset)


def turn_kernel(got, out, chunk, *, levels, half):
    slots = got.shape[0] // 2
    out[0:WIDE, :] = jnp.transpose(dot(picks(slots, 0), got[...], NN)).astype(BF16)
    rest = jnp.transpose(dot(picks(slots, CAP), got[...], NN))
    out[WIDE:VROWS, :] = rest[0 : VROWS - WIDE, :].astype(BF16)
    q, r = iota((slots, 2 * slots), 0), iota((slots, 2 * slots), 1)
    pick = ones_where(r % (2 * CAP) == q % CAP + CAP)
    total = dot(pick, got[:, WIDE - 128 : WIDE], NN)
    first = levels - (LANES - 128) + 4
    lane = iota((slots, 128), 1)
    kept = 128 - first - half
    sums = jnp.where(lane < half, pltpu.roll(total, 128 - first, 1), 0.0)
    chunk[...] = sums + jnp.where(lane < kept, pltpu.roll(total, 128 - first - half, 1), 0.0)


def prep_kernel(first_row, a0, a1, a2, a3, spill, colw, roww, early, late, *, levels):
    refs = (a0, a1, a2, a3)
    tops = jnp.concatenate([ref[VROWS - 16 : VROWS, :].astype(F32) for ref in refs], 1)
    at = levels - (VROWS - 16)
    fr, fc = tops[at : at + 1, :], tops[at + 1 : at + 2, :]
    row, col = tops[at + 2 : at + 3, :].astype(jnp.int32), tops[at + 3 : at + 4, :].astype(jnp.int32)
    n = fr.shape[1]
    cols = iota((GC, n), 0)
    cw = jnp.where(cols == col, 1.0 - fc, jnp.where(cols == col + 1, fc, 0.0)).astype(BF16)
    colw[...] = cw
    rel = iota((BLOCK, n), 0) + first_row[0]
    roww[...] = jnp.where(rel == row, 1.0 - fr, 0.0) + jnp.where(rel == row + 1, fr, 0.0)
    last = jnp.where(row == GR - 1, fr, 0.0)
    part = a0.shape[1]
    out = jnp.zeros((VROWS, GC), F32)
    for j, ref in enumerate(refs):
        cols = slice(j * part, (j + 1) * part)
        early[:, cols] = ref[0 : early.shape[0], :]
        late[:, cols] = ref[early.shape[0] : VROWS, :]
        lhs = (ref[...].astype(F32) * last[:, cols]).astype(BF16)
        out = out + dot(lhs, cw[:, cols], NT)
    spill[...] = out.astype(BF16)


def grid_part(rows, colw, roww, lo, hi):
    lhs = rows[lo:hi, :].astype(F32)[:, None, :] * roww[...][None, :, :]
    lhs = lhs.reshape((hi - lo) * BLOCK, rows.shape[1]).astype(BF16)
    return dot(lhs, colw[...], NT).reshape(hi - lo, BLOCK, GC)


def grid_kernel(rows, colw, roww, out):
    for lo, hi in PARTS[:EARLY]:
        out[lo:hi] = grid_part(rows, colw, roww, lo, hi)


def join_kernel(grid, rows, colw, roww, spill, out, joined, sems):
    levels = out.shape[0]
    split, size = PARTS[EARLY][0], PARTS[EARLY][1] - PARTS[EARLY][0]

    def copy_of(i):
        lo, hi = PARTS[i][0], min(PARTS[i][1], levels)
        return pltpu.make_async_copy(joined.at[pl.ds(lo, hi - lo)], out.at[pl.ds(lo, hi - lo)], sems.at[i])

    def add(own, at, n):
        first = iota((n, BLOCK, GC), 1) == 0
        joined[pl.ds(at, n)] = own + jnp.where(first, spill[pl.ds(at, n), :].astype(F32)[:, None, :], 0.0)

    for i, (lo, hi) in enumerate(PARTS[:EARLY]):
        add(grid[lo:hi], lo, hi - lo)
        copy_of(i).start()

    def later(i, carry):
        lo = pl.multiple_of(i * size, 16)
        lhs = rows[pl.ds(lo, size), :].astype(F32)[:, None, :] * roww[...][None, :, :]
        lhs = lhs.reshape(size * BLOCK, rows.shape[1]).astype(BF16)
        add(dot(lhs, colw[...], NT).reshape(size, BLOCK, GC), pl.multiple_of(split + lo, 16), size)
        for part in range(EARLY, len(PARTS)):

            @pl.when(i == part - EARLY)
            def _():
                copy_of(part).start()

        return carry

    lax.fori_loop(0, len(PARTS) - EARLY, later, 0)
    for i in range(len(PARTS)):
        copy_of(i).wait()


def slot_bias_kernel(got, out, *, half):
    t = jnp.transpose(got[...])
    n = got.shape[0] // 2
    out[0:half, :] = t[0:half, 0:n]
    out[half : 2 * half, :] = t[0:half, n : 2 * n]


def bias_kernel(b0, b1, b2, b3, out, *, scale):
    out[...] = ((b0[...] + b1[...]) + (b2[...] + b3[...])) * scale


VM = pl.BlockSpec(memory_space=pltpu.VMEM)
HBM = pl.BlockSpec(memory_space=pltpu.HBM)


def per_device(
    departure, inv_var, k_matrix, frac_row, frac_col, dest_tile, cell_row, cell_col, predictors, scan_pos
):
    n_tile = lax.axis_size("tile")
    n_slot = lax.axis_size("slot")
    obs, chans, levels = k_matrix.shape
    slots = n_tile * CAP
    params = pltpu.CompilerParams(vmem_limit_bytes=VMEM)
    tight = pltpu.CompilerParams(vmem_limit_bytes=56 * 1024 * 1024)
    steps = 10
    flat = lambda x: x.reshape(1, obs)
    small = (
        departure,
        inv_var.reshape(1, chans),
        flat(dest_tile),
        flat(frac_row),
        flat(frac_col),
        flat(cell_row),
        flat(cell_col),
        predictors.T,
        flat(scan_pos),
    )
    send = pl.pallas_call(
        functools.partial(send_kernel, steps=steps),
        out_shape=jax.ShapeDtypeStruct((2 * slots, WIDE), BF16),
        in_specs=[HBM] * (1 + len(small)),
        out_specs=HBM,
        scratch_shapes=[pltpu.VMEM(x.shape, x.dtype) for x in small]
        + [
            pltpu.VMEM((chans, obs, levels), BF16),
            pltpu.VMEM((obs, LANES), F32),
            pltpu.VMEM((2 * slots, WIDE), BF16),
            pltpu.SemaphoreType.DMA((steps,)),
            pltpu.SemaphoreType.DMA((len(small),)),
            pltpu.SemaphoreType.DMA((OUT_BLOCKS,)),
        ],
        compiler_params=tight,
        name="send",
    )(jnp.transpose(k_matrix, (1, 0, 2)), *small)
    got = lax.all_to_all(send.reshape(n_tile, 2 * CAP, WIDE), "tile", 0, 0, tiled=True).reshape(2 * slots, WIDE)
    turned, chunk = pl.pallas_call(
        functools.partial(turn_kernel, levels=levels, half=chans // 2),
        out_shape=(jax.ShapeDtypeStruct((VROWS, slots), BF16), jax.ShapeDtypeStruct((slots, 128), F32)),
        in_specs=[VM],
        out_specs=(VM, VM),
        compiler_params=params,
        name="turn",
    )(got)

    def around(x, distances):
        return [x] + [lax.ppermute(x, "slot", [(i, (i + d) % n_slot) for i in range(n_slot)]) for d in distances]

    blocks = around(turned, (1, 3, 2))
    chunks = lax.all_to_all(chunk.reshape(n_tile, CAP, 128), "tile", 0, 0, tiled=True).reshape(slots, 128)
    total = n_slot * slots
    split = PARTS[EARLY][0]
    first_row = (lax.axis_index("slot") * BLOCK).astype(jnp.int32).reshape(1)
    spill, colw, roww, early, late = pl.pallas_call(
        functools.partial(prep_kernel, levels=levels),
        out_shape=(
            jax.ShapeDtypeStruct((VROWS, GC), BF16),
            jax.ShapeDtypeStruct((GC, total), BF16),
            jax.ShapeDtypeStruct((BLOCK, total), F32),
            jax.ShapeDtypeStruct((split, total), BF16),
            jax.ShapeDtypeStruct((VROWS - split, total), BF16),
        ),
        in_specs=[pl.BlockSpec(memory_space=pltpu.SMEM)] + [VM] * 4,
        out_specs=(VM,) * 5,
        compiler_params=params,
        name="prep",
    )(first_row, *blocks)
    pairs = [(t * n_slot, ((t + 1) % n_tile) * n_slot) for t in range(n_tile)]
    arrived = lax.ppermute(spill, ("tile", "slot"), pairs)
    own = pl.pallas_call(
        grid_kernel,
        out_shape=jax.ShapeDtypeStruct((split, BLOCK, GC), F32),
        in_specs=[VM] * 3,
        out_specs=VM,
        compiler_params=params,
        name="grid",
    )(early, colw, roww)
    own, chunks = lax.optimization_barrier((own, chunks))
    slot_bias = pl.pallas_call(
        functools.partial(slot_bias_kernel, half=chans // 2),
        out_shape=jax.ShapeDtypeStruct((chans, 128), F32),
        in_specs=[VM],
        out_specs=VM,
        compiler_params=params,
        name="slot_bias",
    )(chunks)
    biases = around(slot_bias, (2, 1, 3))
    grid = pl.pallas_call(
        join_kernel,
        out_shape=jax.ShapeDtypeStruct((levels, BLOCK, GC), F32),
        in_specs=[VM] * 5,
        out_specs=HBM,
        scratch_shapes=[pltpu.VMEM((VROWS, BLOCK, GC), F32), pltpu.SemaphoreType.DMA((len(PARTS),))],
        compiler_params=params,
        name="join",
    )(own, late, colw, roww, arrived)
    *biases, grid = lax.optimization_barrier((*biases, grid))
    bias = pl.pallas_call(
        functools.partial(bias_kernel, scale=1.0 / math.sqrt(obs * n_tile * n_slot)),
        out_shape=jax.ShapeDtypeStruct((chans, 128), F32),
        in_specs=[VM] * 4,
        out_specs=VM,
        compiler_params=params,
        name="bias",
    )(*biases)
    return jnp.transpose(grid, (1, 2, 0)), bias


def solution(mesh):
    both = ("tile", "slot")
    placed = (
        P(both, None),
        P(),
        P(both, None, None),
        P(both),
        P(both),
        P(both, None),
        P(both),
        P(both),
        P(both, None),
        P(both),
    )
    return jax.shard_map(
        per_device,
        mesh=mesh,
        in_specs=placed,
        out_specs=(P(both, None, None), P()),
        check_vma=False,
    )
```

```python
import functools
import math

import jax
import jax.numpy as jnp
from jax import lax
from jax.experimental import pallas as pl
from jax.experimental.pallas import tpu as pltpu
from jax.sharding import PartitionSpec as P

F32 = jnp.float32
BF16 = jnp.bfloat16
NT = (((1,), (1,)), ((), ()))
NN = (((1,), (0,)), ((), ()))

CAP = 4
GR = 32
GC = 256
LANES = 512
WIDE = LANES // 2
VROWS = 416
PARTS = ((0, 128), (128, 256), (256, 336), (336, 416))
EARLY = 2
OUT_BLOCKS = 4
BLOCK = 8
VMEM = 24 * 1024 * 1024


def iota(shape, dim):
    return lax.broadcasted_iota(jnp.int32, shape, dim)


def dot(a, b, dims):
    return lax.dot_general(a, b, dims, preferred_element_type=F32)


def ones_where(mask):
    return jnp.where(mask, 1.0, 0.0).astype(BF16)


def send_kernel(*refs, steps):
    k_hbm, small_hbm, out, small = refs[0], refs[1:10], refs[10], refs[11:20]
    kbuf, acc, placed, sems, small_sems, out_sems = refs[20:]
    chans, obs, levels = k_hbm.shape
    per = chans // steps
    small_copies = [
        pltpu.make_async_copy(src, dst, small_sems.at[i]) for i, (src, dst) in enumerate(zip(small_hbm, small))
    ]
    copies = [
        pltpu.make_async_copy(k_hbm.at[pl.ds(i * per, per)], kbuf.at[pl.ds(i * per, per)], sems.at[i])
        for i in range(steps)
    ]
    for copy in small_copies[:2] + copies[:2] + small_copies[2:] + copies[2:]:
        copy.start()
    dep, inv, tile, frow, fcol, crow, ccol, predt, scan = small
    rows_out = out.shape[0]

    kinds = 128
    half = chans // 2
    base = levels - (LANES - 128)
    first = base + 4
    er, ec = iota((chans, 128), 0), iota((chans, 128), 1)
    qr, qk = iota((rows_out, kinds), 0), iota((rows_out, kinds), 1)
    spreads, places = [], []
    for h in range(2):
        mine = (er >= h * half) & (er < (h + 1) * half)
        e = ones_where((ec == er - h * half + first) & mine)
        f = ones_where((ec == er - h * half + first + half) & mine)
        spreads.append((e, f))
        q = qk + h * kinds
        places.append(ones_where(qr == (q // CAP) * (2 * CAP) + CAP + q % CAP))
    acc[...] = jnp.zeros(acc.shape, F32)
    for copy in small_copies[:2]:
        copy.wait()
    wbf = (dep[...].astype(F32) * inv[...]).astype(BF16)
    w = wbf.astype(F32)

    def sums(i):
        copies[i].wait()
        for r in range(0, obs, 16):
            total = acc[r : r + 16, 0:levels]
            for c in range(i * per, (i + 1) * per):
                total = total + w[r : r + 16, c : c + 1] * kbuf[c, r : r + 16, :].astype(F32)
            acc[r : r + 16, 0:levels] = total

    for i in range(steps - 1):
        sums(i)
    for copy in small_copies[2:]:
        copy.wait()

    tr = jnp.broadcast_to(tile[...].astype(F32), (obs, obs))
    ri, ci = iota((obs, obs), 0), iota((obs, obs), 1)
    tc = jnp.sum(jnp.where(ri == ci, tr, 0.0), 1, keepdims=True)
    rank = jnp.sum(jnp.where((tc == tr) & (ri < ci), 1.0, 0.0), 0, keepdims=True)
    slot = (tile[...].astype(F32) * (2 * CAP) + rank).astype(jnp.int32)
    at = iota((rows_out, obs), 0)
    first_half, second_half = ones_where(at == slot), ones_where(at == slot + CAP)

    rows = iota((128, obs), 0)
    place = jnp.where(rows == base, frow[...].astype(F32), 0.0)
    place = jnp.where(rows == base + 1, fcol[...].astype(F32), place)
    place = jnp.where(rows == base + 2, crow[...].astype(F32), place)
    place = jnp.where(rows == base + 3, ccol[...].astype(F32), place)
    extra = dot(second_half, place.astype(BF16), NT)

    npred = predt.shape[0]
    ind = jnp.where(iota((kinds - npred, obs), 0) == scan[...], 1.0, 0.0)
    basist = jnp.concatenate([predt[...].astype(F32), ind], 0).astype(BF16)
    biast = dot(basist, wbf, NN)
    hi = biast.astype(BF16)
    lo = (biast - hi.astype(F32)).astype(BF16)
    for (e, f), place in zip(spreads, places):
        part = (dot(hi, e, NN) + dot(lo, f, NN)).astype(BF16)
        extra = extra + dot(place, part, NN)

    for i in range(steps - 1, steps):
        sums(i)
    rows = acc[...].astype(BF16)
    size = rows_out // OUT_BLOCKS
    out_copies = []
    for i in range(OUT_BLOCKS):
        at = slice(i * size, (i + 1) * size)
        block = dot(first_half[at, :], rows[:, 0:WIDE], NN) + dot(second_half[at, :], rows[:, WIDE:LANES], NN)
        placed[at, 0 : WIDE - 128] = block[:, 0 : WIDE - 128].astype(BF16)
        placed[at, WIDE - 128 : WIDE] = (block[:, WIDE - 128 : WIDE] + extra[at, :]).astype(BF16)
        here = pl.ds(i * size, size)
        out_copies.append(pltpu.make_async_copy(placed.at[here], out.at[here], out_sems.at[i]))
        out_copies[i].start()
    for copy in out_copies:
        copy.wait()


def picks(slots, offset):
    q, r = iota((slots, 2 * slots), 0), iota((slots, 2 * slots), 1)
    return ones_where(r == (q // CAP) * (2 * CAP) + q % CAP + offset)


def turn_kernel(got, out, chunk, *, levels, half):
    slots = got.shape[0] // 2
    out[0:WIDE, :] = jnp.transpose(dot(picks(slots, 0), got[...], NN)).astype(BF16)
    rest = jnp.transpose(dot(picks(slots, CAP), got[...], NN))
    out[WIDE:VROWS, :] = rest[0 : VROWS - WIDE, :].astype(BF16)
    q, r = iota((slots, 2 * slots), 0), iota((slots, 2 * slots), 1)
    pick = ones_where(r % (2 * CAP) == q % CAP + CAP)
    total = dot(pick, got[:, WIDE - 128 : WIDE], NN)
    first = levels - (LANES - 128) + 4
    lane = iota((slots, 128), 1)
    kept = 128 - first - half
    sums = jnp.where(lane < half, pltpu.roll(total, 128 - first, 1), 0.0)
    chunk[...] = sums + jnp.where(lane < kept, pltpu.roll(total, 128 - first - half, 1), 0.0)


def prep_kernel(first_row, a0, a1, a2, a3, spill, colw, roww, early, late, *, levels):
    refs = (a0, a1, a2, a3)
    tops = jnp.concatenate([ref[VROWS - 16 : VROWS, :].astype(F32) for ref in refs], 1)
    at = levels - (VROWS - 16)
    fr, fc = tops[at : at + 1, :], tops[at + 1 : at + 2, :]
    row, col = tops[at + 2 : at + 3, :].astype(jnp.int32), tops[at + 3 : at + 4, :].astype(jnp.int32)
    n = fr.shape[1]
    cols = iota((GC, n), 0)
    cw = jnp.where(cols == col, 1.0 - fc, jnp.where(cols == col + 1, fc, 0.0)).astype(BF16)
    colw[...] = cw
    rel = iota((BLOCK, n), 0) + first_row[0]
    roww[...] = jnp.where(rel == row, 1.0 - fr, 0.0) + jnp.where(rel == row + 1, fr, 0.0)
    last = jnp.where(row == GR - 1, fr, 0.0)
    part = a0.shape[1]
    out = jnp.zeros((VROWS, GC), F32)
    for j, ref in enumerate(refs):
        cols = slice(j * part, (j + 1) * part)
        early[:, cols] = ref[0 : early.shape[0], :]
        late[:, cols] = ref[early.shape[0] : VROWS, :]
        lhs = (ref[...].astype(F32) * last[:, cols]).astype(BF16)
        out = out + dot(lhs, cw[:, cols], NT)
    spill[...] = out.astype(BF16)


def grid_part(rows, colw, roww, lo, hi):
    lhs = rows[lo:hi, :].astype(F32)[:, None, :] * roww[...][None, :, :]
    lhs = lhs.reshape((hi - lo) * BLOCK, rows.shape[1]).astype(BF16)
    return dot(lhs, colw[...], NT).reshape(hi - lo, BLOCK, GC)


def grid_kernel(rows, colw, roww, out):
    for lo, hi in PARTS[:EARLY]:
        out[lo:hi] = grid_part(rows, colw, roww, lo, hi)


def join_kernel(grid, rows, colw, roww, spill, out, joined, sems):
    levels = out.shape[0]
    split, size = PARTS[EARLY][0], PARTS[EARLY][1] - PARTS[EARLY][0]

    def copy_of(i):
        lo, hi = PARTS[i][0], min(PARTS[i][1], levels)
        return pltpu.make_async_copy(joined.at[pl.ds(lo, hi - lo)], out.at[pl.ds(lo, hi - lo)], sems.at[i])

    def add(own, at, n):
        first = iota((n, BLOCK, GC), 1) == 0
        joined[pl.ds(at, n)] = own + jnp.where(first, spill[pl.ds(at, n), :].astype(F32)[:, None, :], 0.0)

    for i, (lo, hi) in enumerate(PARTS[:EARLY]):
        add(grid[lo:hi], lo, hi - lo)
        copy_of(i).start()

    def later(i, carry):
        lo = pl.multiple_of(i * size, 16)
        lhs = rows[pl.ds(lo, size), :].astype(F32)[:, None, :] * roww[...][None, :, :]
        lhs = lhs.reshape(size * BLOCK, rows.shape[1]).astype(BF16)
        add(dot(lhs, colw[...], NT).reshape(size, BLOCK, GC), pl.multiple_of(split + lo, 16), size)
        for part in range(EARLY, len(PARTS)):

            @pl.when(i == part - EARLY)
            def _():
                copy_of(part).start()

        return carry

    lax.fori_loop(0, len(PARTS) - EARLY, later, 0)
    for i in range(len(PARTS)):
        copy_of(i).wait()


def slot_bias_kernel(got, out, *, half):
    t = jnp.transpose(got[...])
    n = got.shape[0] // 2
    out[0:half, :] = t[0:half, 0:n]
    out[half : 2 * half, :] = t[0:half, n : 2 * n]


def bias_kernel(b0, b1, b2, b3, out, *, scale):
    out[...] = ((b0[...] + b1[...]) + (b2[...] + b3[...])) * scale


VM = pl.BlockSpec(memory_space=pltpu.VMEM)
HBM = pl.BlockSpec(memory_space=pltpu.HBM)


def per_device(
    departure, inv_var, k_matrix, frac_row, frac_col, dest_tile, cell_row, cell_col, predictors, scan_pos
):
    n_tile = lax.axis_size("tile")
    n_slot = lax.axis_size("slot")
    obs, chans, levels = k_matrix.shape
    slots = n_tile * CAP
    params = pltpu.CompilerParams(vmem_limit_bytes=VMEM)
    tight = pltpu.CompilerParams(vmem_limit_bytes=56 * 1024 * 1024)
    steps = 10
    flat = lambda x: x.reshape(1, obs)
    small = (
        departure,
        inv_var.reshape(1, chans),
        flat(dest_tile),
        flat(frac_row),
        flat(frac_col),
        flat(cell_row),
        flat(cell_col),
        predictors.T,
        flat(scan_pos),
    )
    send = pl.pallas_call(
        functools.partial(send_kernel, steps=steps),
        out_shape=jax.ShapeDtypeStruct((2 * slots, WIDE), BF16),
        in_specs=[HBM] * (1 + len(small)),
        out_specs=HBM,
        scratch_shapes=[pltpu.VMEM(x.shape, x.dtype) for x in small]
        + [
            pltpu.VMEM((chans, obs, levels), BF16),
            pltpu.VMEM((obs, LANES), F32),
            pltpu.VMEM((2 * slots, WIDE), BF16),
            pltpu.SemaphoreType.DMA((steps,)),
            pltpu.SemaphoreType.DMA((len(small),)),
            pltpu.SemaphoreType.DMA((OUT_BLOCKS,)),
        ],
        compiler_params=tight,
        name="send",
    )(jnp.transpose(k_matrix, (1, 0, 2)), *small)
    got = lax.all_to_all(send.reshape(n_tile, 2 * CAP, WIDE), "tile", 0, 0, tiled=True).reshape(2 * slots, WIDE)
    turned, chunk = pl.pallas_call(
        functools.partial(turn_kernel, levels=levels, half=chans // 2),
        out_shape=(jax.ShapeDtypeStruct((VROWS, slots), BF16), jax.ShapeDtypeStruct((slots, 128), F32)),
        in_specs=[VM],
        out_specs=(VM, VM),
        compiler_params=params,
        name="turn",
    )(got)

    def around(x, distances):
        return [x] + [lax.ppermute(x, "slot", [(i, (i + d) % n_slot) for i in range(n_slot)]) for d in distances]

    blocks = around(turned, (1, 3, 2))
    chunks = lax.all_to_all(chunk.reshape(n_tile, CAP, 128), "tile", 0, 0, tiled=True).reshape(slots, 128)
    total = n_slot * slots
    split = PARTS[EARLY][0]
    first_row = (lax.axis_index("slot") * BLOCK).astype(jnp.int32).reshape(1)
    spill, colw, roww, early, late = pl.pallas_call(
        functools.partial(prep_kernel, levels=levels),
        out_shape=(
            jax.ShapeDtypeStruct((VROWS, GC), BF16),
            jax.ShapeDtypeStruct((GC, total), BF16),
            jax.ShapeDtypeStruct((BLOCK, total), F32),
            jax.ShapeDtypeStruct((split, total), BF16),
            jax.ShapeDtypeStruct((VROWS - split, total), BF16),
        ),
        in_specs=[pl.BlockSpec(memory_space=pltpu.SMEM)] + [VM] * 4,
        out_specs=(VM,) * 5,
        compiler_params=params,
        name="prep",
    )(first_row, *blocks)
    pairs = [(t * n_slot, ((t + 1) % n_tile) * n_slot) for t in range(n_tile)]
    arrived = lax.ppermute(spill, ("tile", "slot"), pairs)
    own = pl.pallas_call(
        grid_kernel,
        out_shape=jax.ShapeDtypeStruct((split, BLOCK, GC), F32),
        in_specs=[VM] * 3,
        out_specs=VM,
        compiler_params=params,
        name="grid",
    )(early, colw, roww)
    own, chunks = lax.optimization_barrier((own, chunks))
    slot_bias = pl.pallas_call(
        functools.partial(slot_bias_kernel, half=chans // 2),
        out_shape=jax.ShapeDtypeStruct((chans, 128), F32),
        in_specs=[VM],
        out_specs=VM,
        compiler_params=params,
        name="slot_bias",
    )(chunks)
    biases = around(slot_bias, (2, 1, 3))
    grid = pl.pallas_call(
        join_kernel,
        out_shape=jax.ShapeDtypeStruct((levels, BLOCK, GC), F32),
        in_specs=[VM] * 5,
        out_specs=HBM,
        scratch_shapes=[pltpu.VMEM((VROWS, BLOCK, GC), F32), pltpu.SemaphoreType.DMA((len(PARTS),))],
        compiler_params=params,
        name="join",
    )(own, late, colw, roww, arrived)
    *biases, grid = lax.optimization_barrier((*biases, grid))
    bias = pl.pallas_call(
        functools.partial(bias_kernel, scale=1.0 / math.sqrt(obs * n_tile * n_slot)),
        out_shape=jax.ShapeDtypeStruct((chans, 128), F32),
        in_specs=[VM] * 4,
        out_specs=VM,
        compiler_params=params,
        name="bias",
    )(*biases)
    return jnp.transpose(grid, (1, 2, 0)), bias


def solution(mesh):
    both = ("tile", "slot")
    placed = (
        P(both, None),
        P(),
        P(both, None, None),
        P(both),
        P(both),
        P(both, None),
        P(both),
        P(both),
        P(both, None),
        P(both),
    )
    return jax.shard_map(
        per_device,
        mesh=mesh,
        in_specs=placed,
        out_specs=(P(both, None, None), P()),
        check_vma=False,
    )
```

```python
import functools
import math

import jax
import jax.numpy as jnp
from jax import lax
from jax.experimental import pallas as pl
from jax.experimental.pallas import tpu as pltpu
from jax.sharding import PartitionSpec as P

F32 = jnp.float32
BF16 = jnp.bfloat16
NT = (((1,), (1,)), ((), ()))
NN = (((1,), (0,)), ((), ()))

CAP = 4
GR = 32
GC = 256
LANES = 512
WIDE = LANES // 2
VROWS = 416
PARTS = ((0, 128), (128, 256), (256, 336), (336, 416))
EARLY = 2
OUT_BLOCKS = 4
BLOCK = 8
VMEM = 24 * 1024 * 1024


def iota(shape, dim):
    return lax.broadcasted_iota(jnp.int32, shape, dim)


def dot(a, b, dims):
    return lax.dot_general(a, b, dims, preferred_element_type=F32)


def ones_where(mask):
    return jnp.where(mask, 1.0, 0.0).astype(BF16)


def send_kernel(*refs, steps):
    k_hbm, small_hbm, out, small = refs[0], refs[1:10], refs[10], refs[11:20]
    kbuf, acc, placed, sems, small_sems, out_sems = refs[20:]
    chans, obs, levels = k_hbm.shape
    per = chans // steps
    small_copies = [
        pltpu.make_async_copy(src, dst, small_sems.at[i]) for i, (src, dst) in enumerate(zip(small_hbm, small))
    ]
    copies = [
        pltpu.make_async_copy(k_hbm.at[pl.ds(i * per, per)], kbuf.at[pl.ds(i * per, per)], sems.at[i])
        for i in range(steps)
    ]
    for copy in small_copies[:2] + copies[:2] + small_copies[2:] + copies[2:]:
        copy.start()
    dep, inv, tile, frow, fcol, crow, ccol, predt, scan = small
    rows_out = out.shape[0]

    kinds = 128
    half = chans // 2
    base = levels - (LANES - 128)
    first = base + 4
    er, ec = iota((chans, 128), 0), iota((chans, 128), 1)
    qr, qk = iota((rows_out, kinds), 0), iota((rows_out, kinds), 1)
    spreads, places = [], []
    for h in range(2):
        mine = (er >= h * half) & (er < (h + 1) * half)
        e = ones_where((ec == er - h * half + first) & mine)
        f = ones_where((ec == er - h * half + first + half) & mine)
        spreads.append((e, f))
        q = qk + h * kinds
        places.append(ones_where(qr == (q // CAP) * (2 * CAP) + CAP + q % CAP))
    acc[...] = jnp.zeros(acc.shape, F32)
    for copy in small_copies[:2]:
        copy.wait()
    wbf = (dep[...].astype(F32) * inv[...]).astype(BF16)
    w = wbf.astype(F32)

    def sums(i):
        copies[i].wait()
        for r in range(0, obs, 16):
            total = acc[r : r + 16, 0:levels]
            for c in range(i * per, (i + 1) * per):
                total = total + w[r : r + 16, c : c + 1] * kbuf[c, r : r + 16, :].astype(F32)
            acc[r : r + 16, 0:levels] = total

    for i in range(steps - 1):
        sums(i)
    for copy in small_copies[2:]:
        copy.wait()

    tr = jnp.broadcast_to(tile[...].astype(F32), (obs, obs))
    ri, ci = iota((obs, obs), 0), iota((obs, obs), 1)
    tc = jnp.sum(jnp.where(ri == ci, tr, 0.0), 1, keepdims=True)
    rank = jnp.sum(jnp.where((tc == tr) & (ri < ci), 1.0, 0.0), 0, keepdims=True)
    slot = (tile[...].astype(F32) * (2 * CAP) + rank).astype(jnp.int32)
    at = iota((rows_out, obs), 0)
    first_half, second_half = ones_where(at == slot), ones_where(at == slot + CAP)

    rows = iota((128, obs), 0)
    place = jnp.where(rows == base, frow[...].astype(F32), 0.0)
    place = jnp.where(rows == base + 1, fcol[...].astype(F32), place)
    place = jnp.where(rows == base + 2, crow[...].astype(F32), place)
    place = jnp.where(rows == base + 3, ccol[...].astype(F32), place)
    extra = dot(second_half, place.astype(BF16), NT)

    npred = predt.shape[0]
    ind = jnp.where(iota((kinds - npred, obs), 0) == scan[...], 1.0, 0.0)
    basist = jnp.concatenate([predt[...].astype(F32), ind], 0).astype(BF16)
    biast = dot(basist, wbf, NN)
    hi = biast.astype(BF16)
    lo = (biast - hi.astype(F32)).astype(BF16)
    for (e, f), place in zip(spreads, places):
        part = (dot(hi, e, NN) + dot(lo, f, NN)).astype(BF16)
        extra = extra + dot(place, part, NN)

    for i in range(steps - 1, steps):
        sums(i)
    rows = acc[...].astype(BF16)
    size = rows_out // OUT_BLOCKS
    out_copies = []
    for i in range(OUT_BLOCKS):
        at = slice(i * size, (i + 1) * size)
        block = dot(first_half[at, :], rows[:, 0:WIDE], NN) + dot(second_half[at, :], rows[:, WIDE:LANES], NN)
        placed[at, 0 : WIDE - 128] = block[:, 0 : WIDE - 128].astype(BF16)
        placed[at, WIDE - 128 : WIDE] = (block[:, WIDE - 128 : WIDE] + extra[at, :]).astype(BF16)
        here = pl.ds(i * size, size)
        out_copies.append(pltpu.make_async_copy(placed.at[here], out.at[here], out_sems.at[i]))
        out_copies[i].start()
    for copy in out_copies:
        copy.wait()


def picks(slots, offset):
    q, r = iota((slots, 2 * slots), 0), iota((slots, 2 * slots), 1)
    return ones_where(r == (q // CAP) * (2 * CAP) + q % CAP + offset)


def turn_kernel(got, out, chunk, *, levels, half):
    slots = got.shape[0] // 2
    out[0:WIDE, :] = jnp.transpose(dot(picks(slots, 0), got[...], NN)).astype(BF16)
    rest = jnp.transpose(dot(picks(slots, CAP), got[...], NN))
    out[WIDE:VROWS, :] = rest[0 : VROWS - WIDE, :].astype(BF16)
    q, r = iota((slots, 2 * slots), 0), iota((slots, 2 * slots), 1)
    pick = ones_where(r % (2 * CAP) == q % CAP + CAP)
    total = dot(pick, got[:, WIDE - 128 : WIDE], NN)
    first = levels - (LANES - 128) + 4
    lane = iota((slots, 128), 1)
    kept = 128 - first - half
    sums = jnp.where(lane < half, pltpu.roll(total, 128 - first, 1), 0.0)
    chunk[...] = sums + jnp.where(lane < kept, pltpu.roll(total, 128 - first - half, 1), 0.0)


def prep_kernel(first_row, a0, a1, a2, a3, spill, colw, roww, early, late, *, levels):
    refs = (a0, a1, a2, a3)
    tops = jnp.concatenate([ref[VROWS - 16 : VROWS, :].astype(F32) for ref in refs], 1)
    at = levels - (VROWS - 16)
    fr, fc = tops[at : at + 1, :], tops[at + 1 : at + 2, :]
    row, col = tops[at + 2 : at + 3, :].astype(jnp.int32), tops[at + 3 : at + 4, :].astype(jnp.int32)
    n = fr.shape[1]
    cols = iota((GC, n), 0)
    cw = jnp.where(cols == col, 1.0 - fc, jnp.where(cols == col + 1, fc, 0.0)).astype(BF16)
    colw[...] = cw
    rel = iota((BLOCK, n), 0) + first_row[0]
    roww[...] = jnp.where(rel == row, 1.0 - fr, 0.0) + jnp.where(rel == row + 1, fr, 0.0)
    last = jnp.where(row == GR - 1, fr, 0.0)
    part = a0.shape[1]
    out = jnp.zeros((VROWS, GC), F32)
    for j, ref in enumerate(refs):
        cols = slice(j * part, (j + 1) * part)
        early[:, cols] = ref[0 : early.shape[0], :]
        late[:, cols] = ref[early.shape[0] : VROWS, :]
        lhs = (ref[...].astype(F32) * last[:, cols]).astype(BF16)
        out = out + dot(lhs, cw[:, cols], NT)
    spill[...] = out.astype(BF16)


def grid_part(rows, colw, roww, lo, hi):
    lhs = rows[lo:hi, :].astype(F32)[:, None, :] * roww[...][None, :, :]
    lhs = lhs.reshape((hi - lo) * BLOCK, rows.shape[1]).astype(BF16)
    return dot(lhs, colw[...], NT).reshape(hi - lo, BLOCK, GC)


def grid_kernel(rows, colw, roww, out):
    for lo, hi in PARTS[:EARLY]:
        out[lo:hi] = grid_part(rows, colw, roww, lo, hi)


def join_kernel(grid, rows, colw, roww, spill, out, joined, sems):
    levels = out.shape[0]
    split, size = PARTS[EARLY][0], PARTS[EARLY][1] - PARTS[EARLY][0]

    def copy_of(i):
        lo, hi = PARTS[i][0], min(PARTS[i][1], levels)
        return pltpu.make_async_copy(joined.at[pl.ds(lo, hi - lo)], out.at[pl.ds(lo, hi - lo)], sems.at[i])

    def add(own, at, n):
        first = iota((n, BLOCK, GC), 1) == 0
        joined[pl.ds(at, n)] = own + jnp.where(first, spill[pl.ds(at, n), :].astype(F32)[:, None, :], 0.0)

    for i, (lo, hi) in enumerate(PARTS[:EARLY]):
        add(grid[lo:hi], lo, hi - lo)
        copy_of(i).start()

    def later(i, carry):
        lo = pl.multiple_of(i * size, 16)
        lhs = rows[pl.ds(lo, size), :].astype(F32)[:, None, :] * roww[...][None, :, :]
        lhs = lhs.reshape(size * BLOCK, rows.shape[1]).astype(BF16)
        add(dot(lhs, colw[...], NT).reshape(size, BLOCK, GC), pl.multiple_of(split + lo, 16), size)
        for part in range(EARLY, len(PARTS)):

            @pl.when(i == part - EARLY)
            def _():
                copy_of(part).start()

        return carry

    lax.fori_loop(0, len(PARTS) - EARLY, later, 0)
    for i in range(len(PARTS)):
        copy_of(i).wait()


def slot_bias_kernel(got, out, *, half):
    t = jnp.transpose(got[...])
    n = got.shape[0] // 2
    out[0:half, :] = t[0:half, 0:n]
    out[half : 2 * half, :] = t[0:half, n : 2 * n]


def bias_kernel(b0, b1, b2, b3, out, *, scale):
    out[...] = ((b0[...] + b1[...]) + (b2[...] + b3[...])) * scale


VM = pl.BlockSpec(memory_space=pltpu.VMEM)
HBM = pl.BlockSpec(memory_space=pltpu.HBM)


def per_device(
    departure, inv_var, k_matrix, frac_row, frac_col, dest_tile, cell_row, cell_col, predictors, scan_pos
):
    n_tile = lax.axis_size("tile")
    n_slot = lax.axis_size("slot")
    obs, chans, levels = k_matrix.shape
    slots = n_tile * CAP
    params = pltpu.CompilerParams(vmem_limit_bytes=VMEM)
    tight = pltpu.CompilerParams(vmem_limit_bytes=56 * 1024 * 1024)
    steps = 10
    flat = lambda x: x.reshape(1, obs)
    small = (
        departure,
        inv_var.reshape(1, chans),
        flat(dest_tile),
        flat(frac_row),
        flat(frac_col),
        flat(cell_row),
        flat(cell_col),
        predictors.T,
        flat(scan_pos),
    )
    send = pl.pallas_call(
        functools.partial(send_kernel, steps=steps),
        out_shape=jax.ShapeDtypeStruct((2 * slots, WIDE), BF16),
        in_specs=[HBM] * (1 + len(small)),
        out_specs=HBM,
        scratch_shapes=[pltpu.VMEM(x.shape, x.dtype) for x in small]
        + [
            pltpu.VMEM((chans, obs, levels), BF16),
            pltpu.VMEM((obs, LANES), F32),
            pltpu.VMEM((2 * slots, WIDE), BF16),
            pltpu.SemaphoreType.DMA((steps,)),
            pltpu.SemaphoreType.DMA((len(small),)),
            pltpu.SemaphoreType.DMA((OUT_BLOCKS,)),
        ],
        compiler_params=tight,
        name="send",
    )(jnp.transpose(k_matrix, (1, 0, 2)), *small)
    got = lax.all_to_all(send.reshape(n_tile, 2 * CAP, WIDE), "tile", 0, 0, tiled=True).reshape(2 * slots, WIDE)
    turned, chunk = pl.pallas_call(
        functools.partial(turn_kernel, levels=levels, half=chans // 2),
        out_shape=(jax.ShapeDtypeStruct((VROWS, slots), BF16), jax.ShapeDtypeStruct((slots, 128), F32)),
        in_specs=[VM],
        out_specs=(VM, VM),
        compiler_params=params,
        name="turn",
    )(got)

    def around(x, distances):
        return [x] + [lax.ppermute(x, "slot", [(i, (i + d) % n_slot) for i in range(n_slot)]) for d in distances]

    blocks = around(turned, (1, 3, 2))
    chunks = lax.all_to_all(chunk.reshape(n_tile, CAP, 128), "tile", 0, 0, tiled=True).reshape(slots, 128)
    total = n_slot * slots
    split = PARTS[EARLY][0]
    first_row = (lax.axis_index("slot") * BLOCK).astype(jnp.int32).reshape(1)
    spill, colw, roww, early, late = pl.pallas_call(
        functools.partial(prep_kernel, levels=levels),
        out_shape=(
            jax.ShapeDtypeStruct((VROWS, GC), BF16),
            jax.ShapeDtypeStruct((GC, total), BF16),
            jax.ShapeDtypeStruct((BLOCK, total), F32),
            jax.ShapeDtypeStruct((split, total), BF16),
            jax.ShapeDtypeStruct((VROWS - split, total), BF16),
        ),
        in_specs=[pl.BlockSpec(memory_space=pltpu.SMEM)] + [VM] * 4,
        out_specs=(VM,) * 5,
        compiler_params=params,
        name="prep",
    )(first_row, *blocks)
    pairs = [(t * n_slot, ((t + 1) % n_tile) * n_slot) for t in range(n_tile)]
    arrived = lax.ppermute(spill, ("tile", "slot"), pairs)
    own = pl.pallas_call(
        grid_kernel,
        out_shape=jax.ShapeDtypeStruct((split, BLOCK, GC), F32),
        in_specs=[VM] * 3,
        out_specs=VM,
        compiler_params=params,
        name="grid",
    )(early, colw, roww)
    own, chunks = lax.optimization_barrier((own, chunks))
    slot_bias = pl.pallas_call(
        functools.partial(slot_bias_kernel, half=chans // 2),
        out_shape=jax.ShapeDtypeStruct((chans, 128), F32),
        in_specs=[VM],
        out_specs=VM,
        compiler_params=params,
        name="slot_bias",
    )(chunks)
    biases = around(slot_bias, (1, 3, 2))
    grid = pl.pallas_call(
        join_kernel,
        out_shape=jax.ShapeDtypeStruct((levels, BLOCK, GC), F32),
        in_specs=[VM] * 5,
        out_specs=HBM,
        scratch_shapes=[pltpu.VMEM((VROWS, BLOCK, GC), F32), pltpu.SemaphoreType.DMA((len(PARTS),))],
        compiler_params=params,
        name="join",
    )(own, late, colw, roww, arrived)
    *biases, grid = lax.optimization_barrier((*biases, grid))
    bias = pl.pallas_call(
        functools.partial(bias_kernel, scale=1.0 / math.sqrt(obs * n_tile * n_slot)),
        out_shape=jax.ShapeDtypeStruct((chans, 128), F32),
        in_specs=[VM] * 4,
        out_specs=VM,
        compiler_params=params,
        name="bias",
    )(*biases)
    return jnp.transpose(grid, (1, 2, 0)), bias


def solution(mesh):
    both = ("tile", "slot")
    placed = (
        P(both, None),
        P(),
        P(both, None, None),
        P(both),
        P(both),
        P(both, None),
        P(both),
        P(both),
        P(both, None),
        P(both),
    )
    return jax.shard_map(
        per_device,
        mesh=mesh,
        in_specs=placed,
        out_specs=(P(both, None, None), P()),
        check_vma=False,
    )
```
